256 devices in a mesh: pop: 64 (over z, y_lo, x), wa: 4 (over y_hi, core).
Axes of the slice: x: 4, y: 4 (y_hi: 2, y_lo: 2; y = y_hi * 2 + y_lo), z: 8, core: 2. Of those that a mesh axis runs over, the one named last changes fastest.
Arguments:
- left_factors: bfloat16 [24576, 4, 1024], P('pop', None, 'wa'), may hold values from -16 to 16
- right_factors: bfloat16 [24576, 4, 4096], P('pop', None, 'wa'), may hold values from -6 to 6
- fitness_rank: int32 [24576], P('pop'), may hold values from 0 to 24575, each once
- sign_index: int32 [24576], P('pop'), may hold values 0 or 1
- master: float32 [1024, 4096], P(('wa', 'pop')), may hold values from -6 to 6
- moment: float32 [1024, 4096], P(('wa', 'pop')), may hold values from -6 to 6
- second: float32 [1024, 4096], P(('wa', 'pop')), may hold values from 0.5 to 2
Outputs:
- new_master: float32 [1024, 4096], P(('wa', 'pop'))
- new_moment: float32 [1024, 4096], P(('wa', 'pop'))
- new_second: float32 [1024, 4096], P(('wa', 'pop'))
- weights: bfloat16 [1024, 4096], P('wa')
The draws below stay inside these ranges and needn't reach their ends.
Inputs may be any that keep to these rules, and one draw needn't show every extreme that they name: fitness_rank holds each of 0 to 24575 once.
All inputs are finite; a program needn't handle non-finite values. No bound on the sum of `sign_index` on one device may be relied on, other than what follows from the above.
Results may differ from the reference program's by a relative error of at most 0.0023.
Values may be sent and summed in bfloat16 or wider, within the bound.
A program may use at most 64 MiB of HBM per device.

```python
import math
import jax
import jax.numpy as jnp
from jax import lax

D = 4096
ROWS = 1024
R = 4
STEP = 3
MEM_DEV = 384
POP = 24576
N_POP = 64


def with_ends(entries, rng, low, high):
    extent = entries.shape
    place = [jax.random.randint(jax.random.fold_in(rng, axis), (), 0, extent[axis]) for axis in range(len(extent))]
    entries = entries.at[tuple(place)].set(low)
    longest = extent.index(max(extent))
    place[longest] = (place[longest] + 1) % extent[longest]
    return entries.at[tuple(place)].set(high)


def strengthened(entries, stream_key, source, target, blocks, factor):
    owner, partner = [(jnp.arange(entries.shape[dim]) // (entries.shape[dim] // blocks)).reshape([-1 if axis == dim else 1 for axis in range(entries.ndim)]) for dim in (source, target)]
    chosen = jax.random.permutation(stream_key, blocks)[partner]
    strong = (owner == chosen) | (owner == (partner + blocks // 2) % blocks)
    return jnp.where(strong, factor * entries, entries)


def steps_of(stream_key, dims, cuts, least, largest):
    factor_of, own = 1.0, jax.random.fold_in(stream_key, 6)
    for position, blocks in cuts:
        heights = jnp.exp(jax.random.uniform(jax.random.fold_in(own, position), (blocks,), jnp.float32, least / len(cuts), largest / len(cuts)))
        factor_of = factor_of * jnp.repeat(heights, dims[position] // blocks).reshape([-1 if axis == position else 1 for axis in range(len(dims))])
    return factor_of


def bell_draw(stream_key, extent, spread, bound, split=(), held_as=jnp.bfloat16):
    level = steps_of(stream_key, extent, split, -0.22, 0.18) if split else 1.0
    array = jax.random.normal(stream_key, extent, jnp.float32) * spread * level
    return jnp.minimum(jnp.maximum(array, -bound), bound).astype(held_as)


def noise_with(stream_key, extent, width, bound, split, heavy, dtype=jnp.bfloat16):
    values = width * jax.random.normal(stream_key, extent, jnp.float32)
    if split:
        values = values * steps_of(stream_key, extent, split, -0.22, 0.18)
    return jnp.clip(strengthened(values, jax.random.fold_in(stream_key, 3), *heavy), -bound, bound).astype(dtype)


def setup_inputs(seed: int = 0) -> dict:
    keys = jax.random.split(jax.random.key(seed), 8)
    return {
        "left_factors": noise_with(keys[0], (POP, R, ROWS), 1.0, 16.0, ((0, 64), (2, 4)), (0, 2, 64, 4.0)),
        "right_factors": bell_draw(keys[1], (POP, R, D), 1.0, 6.0, ((0, 64), (2, 4))),
        "fitness_rank": jax.random.permutation(keys[2], POP).astype(jnp.int32),
        "sign_index": with_ends((jax.random.randint(keys[3], (POP,), 0, 2) < 1).astype(jnp.int32), jax.random.fold_in(keys[3], 1), 0, 1),
        "master": bell_draw(keys[4], (ROWS, D), 1.0, 6.0, ((0, 256),), jnp.float32),
        "moment": bell_draw(keys[5], (ROWS, D), 1.0, 6.0, ((0, 256),), jnp.float32),
        "second": jnp.clip(jnp.exp(math.log(2.0) - 1.3862944 * jax.random.uniform(keys[6], (ROWS, D), jnp.float32) ** steps_of(keys[6], (ROWS, D), ((0, 256),), -0.2, 0.2)), 0.5, 2.0),
    }


def reference(left_factors, right_factors, fitness_rank, sign_index, master, moment, second):
    population = fitness_rank.shape[0]
    square_sum = population * (population + 1) / (3.0 * (population - 1))
    fitness = (2.0 * fitness_rank.astype(jnp.float32) / (population - 1) - 1.0) * (1.0 - 2.0 * sign_index.astype(jnp.float32))
    fitness = fitness / jnp.sqrt(jnp.float32(square_sum * R))
    scaled = (left_factors * fitness[:, None, None]).astype(jnp.bfloat16)
    row_count = left_factors.shape[2]
    col_count = right_factors.shape[2]
    left_blocks = scaled.reshape(N_POP, MEM_DEV * R, row_count)
    right_blocks = right_factors.reshape(N_POP, MEM_DEV * R, col_count)

    def accumulate(total, pair):
        left_part = pair[0].astype(jnp.float32)
        right_part = pair[1].astype(jnp.float32)
        product = lax.dot_general(left_part, right_part, (((0,), (0,)), ((), ())), precision=lax.Precision.HIGHEST, preferred_element_type=jnp.float32)
        return (total + product, None)
    gradient, _ = lax.scan(accumulate, jnp.zeros((row_count, col_count), jnp.float32), (left_blocks, right_blocks))
    new_moment = 0.8 * moment + 0.2 * gradient
    new_second = 0.95 * second + 0.05 * gradient * gradient
    correct_one = 1.0 - 0.8 ** STEP
    correct_two = 1.0 - 0.95 ** STEP
    new_master = master - 0.3 * (new_moment / correct_one) / (jnp.sqrt(new_second / correct_two) + 1e-08)
    return (new_master, new_moment, new_second, new_master.astype(jnp.bfloat16))
```

```python
import math

import jax
import jax.numpy as jnp
from jax import lax
from jax.experimental import pallas as pl
from jax.experimental.pallas import tpu as pltpu
from jax.sharding import PartitionSpec as P

R = 4
STEP = 3
NZ, NYL, NX = 8, 2, 4
MESH = pl.DeviceIdType.MESH
F32 = jnp.float32
BF16 = jnp.bfloat16


def kernel(
    left_hbm, right_hbm, rank_ref, sign_ref, master_hbm, moment_hbm, second_hbm,
    out_master, out_moment, out_second, out_weights,
    left_raw, left_scaled, right, scale, adam_in,
    grad_p, grad_q, recv_p1, recv_p2, recv_q1, recv_q2, recv_y,
    state_send, state_recv, result_send, result_recv, rows_f32,
    gather_p, gather_q,
    send_sems, recv_sems, local_sems,
):
    members = rank_ref.shape[0]
    depth = members * R
    pop = lax.axis_index("pop")
    wa = lax.axis_index("wa")
    z, yl, x = pop // (NYL * NX), lax.rem(pop // NX, NYL), lax.rem(pop, NX)
    yh, core = wa // 2, lax.rem(wa, 2)
    population = members * NZ * NYL * NX

    def flip(bit, by):
        return 1 - bit if by else bit

    def device(z_, yl_, x_, yh_, core_):
        return (z_ * (NYL * NX) + yl_ * NX + x_, yh_ * 2 + core_)

    def z_peer(step):
        return device(lax.rem(z + step + NZ, NZ), yl, x, yh, core)

    def x_peer(step):
        return device(z, yl, lax.rem(x + step + NX, NX), yh, core)

    def y_peer(phase, part, half):
        return device(z, flip(yl, half), x, flip(yh, phase), flip(core, part))

    others = [(a, b, c) for a in range(2) for b in range(2) for c in range(2) if a + b + c]
    peers = [z_peer(1), z_peer(-1)] + [x_peer(k) for k in (1, 2, 3)]
    peers += [y_peer(*o) for o in others]

    messages = []

    def send(src, dst, to):
        index = len(messages)
        message = pltpu.make_async_remote_copy(
            src_ref=src, dst_ref=dst, send_sem=send_sems.at[index],
            recv_sem=recv_sems.at[index], device_id=to, device_id_type=MESH,
        )
        message.start()
        messages.append(message)
        return message

    left_view = left_hbm.reshape(depth, left_hbm.shape[2])
    right_view = right_hbm.reshape(depth, right_hbm.shape[2])
    load_left = pltpu.make_async_copy(left_view, left_raw.at[0], local_sems.at[0])
    load_left.start()
    load_right = []
    for c in range(NX):
        load_right.append(
            pltpu.make_async_copy(
                right_view.at[:, pl.ds(c * 256, 256)], right.at[c], local_sems.at[1 + c]
            )
        )
    load_state = [
        pltpu.make_async_copy(ref, adam_in.at[a], local_sems.at[5 + a])
        for a, ref in enumerate((master_hbm, moment_hbm, second_hbm))
    ]

    barrier = pltpu.get_barrier_semaphore()
    for peer in peers:
        pl.semaphore_signal(barrier, inc=1, device_id=peer, device_id_type=MESH)
    pl.semaphore_wait(barrier, len(peers))

    to_chip = send(left_view, left_raw.at[2], y_peer(1, 0, 0))
    to_core = send(left_view, left_raw.at[1], y_peer(0, 1, 0))
    for copy in load_right + load_state:
        copy.start()

    square_sum = population * (population + 1) / (3.0 * (population - 1))
    norm = 1.0 / ((population - 1) * math.sqrt(square_sum * R))
    upper = lax.broadcasted_iota(jnp.int32, (8, 128), 0) < R

    def fill(j, _):
        def centred(m):
            return (2 * rank_ref[m] - (population - 1)) * (1 - 2 * sign_ref[m])

        first, second_ = centred(2 * j), centred(2 * j + 1)
        both = jnp.where(upper, jnp.full((8, 128), first), jnp.full((8, 128), second_))
        scale[pl.ds(pl.multiple_of(8 * j, 8), 8), :] = both.astype(F32) * norm
        return 0

    lax.fori_loop(0, members // 2, fill, 0)

    def product(slot, phase, part):
        def scaling(k, _):
            rows = pl.ds(pl.multiple_of(k * 128, 128), 128)
            factor = scale[rows, :]
            for half in range(2):
                cols = pl.ds(half * 128, 128)
                left_scaled[slot, rows, cols] = (
                    left_raw[slot, rows, cols].astype(F32) * factor
                ).astype(BF16)
            return 0

        lax.fori_loop(0, depth // 128, scaling, 0)

        def columns(c, _):
            block = lax.dot_general(
                left_scaled[slot], right[c], (((0,), (0,)), ((), ())),
                preferred_element_type=F32,
            )
            for zz in range(NZ):
                for yy in range(NYL):
                    half = 1 - yl if yy else yl
                    at = zz * 32 + yy * 16
                    piece = block[at : at + 16, :]
                    if part == 0:
                        grad_p[phase, half, zz, c] = piece
                    else:
                        grad_q[phase, half, c, zz] = piece
            return 0

        lax.fori_loop(0, NX, columns, 0)

    def ring_sum(chunks, slots, first_slot, size, me, peer, half):
        long = 1 if half == 0 else -1
        lanes = []
        slot = first_slot
        for direction in (long, -long):
            steps = size // 2 if direction == long else size // 2 - 1
            lanes.append((direction, steps, slot))
            slot += steps
        pending = {}

        def chunk(direction, distance):
            return lax.rem(me + direction * distance + size, size)

        for direction, steps, slot in lanes:
            pending[direction] = send(
                chunks.at[chunk(direction, steps)], slots.at[slot], peer(direction)
            )
        yield
        for j in range(1, size // 2 + 1):
            for direction, steps, slot in lanes:
                if j > steps:
                    continue
                pending[direction].wait_recv()
                target = chunk(direction, steps - j)
                chunks[target] = chunks[target] + slots[slot + j - 1]
                if j < steps:
                    pending[direction] = send(
                        chunks.at[target], slots.at[slot + j], peer(direction)
                    )
            yield

    exchanged = {}

    def reduction(phase, part, half):
        if part == 0:
            own = grad_p.at[phase, half]
            yield from ring_sum(own, recv_p1.at[phase, half], 0, NZ, z, z_peer, half)
            own = own.at[z]
            yield from ring_sum(own, recv_p2.at[phase, half], 0, NX, x, x_peer, half)
            own = own.at[x]
        else:
            own = grad_q.at[phase, half]
            yield from ring_sum(own, recv_q1.at[phase, half], 0, NX, x, x_peer, half)
            own = own.at[x]
            yield from ring_sum(own, recv_q2.at[phase, half], 0, NZ, z, z_peer, half)
            own = own.at[z]
        if phase + part + half:
            exchanged[phase, part, half] = send(
                own, recv_y.at[phase, part, half], y_peer(phase, part, half)
            )

    def run(tasks):
        while tasks:
            alive = []
            for task in tasks:
                try:
                    next(task)
                    alive.append(task)
                except StopIteration:
                    pass
            tasks = alive

    def begin(phase, part):
        tasks = [reduction(phase, part, half) for half in range(2)]
        for task in tasks:
            next(task)
        return tasks

    load_left.wait()
    for copy in load_right:
        copy.wait()
    product(0, 0, 0)
    tasks = begin(0, 0)
    to_core.wait_recv()
    product(1, 0, 1)
    tasks += begin(0, 1)

    for copy in load_state:
        copy.wait()
    for xx in range(NX):
        for w in range(4):
            for a in range(3):
                state_send[xx, w, a] = adam_in[a, :, pl.ds(w * 1024 + xx * 256, 256)]
    state_recv[x] = state_send[x]
    state = []
    for k in (1, 2, 3):
        state.append(send(state_send.at[lax.rem(x + k, NX)], state_recv.at[x], x_peer(k)))

    to_chip.wait_recv()
    to_core2 = send(left_raw.at[2], left_raw.at[3], y_peer(0, 1, 0))
    run(tasks)
    product(2, 1, 0)
    tasks = begin(1, 0)
    to_core2.wait_recv()
    product(3, 1, 1)
    tasks += begin(1, 1)
    run(tasks)

    for message in state:
        message.wait_recv()
    for message in exchanged.values():
        message.wait_recv()
    correct_one = 1.0 - 0.8**STEP
    correct_two = 1.0 - 0.95**STEP
    gathered = []
    for phase in range(2):
        for part in range(2):
            owner = flip(yh, phase) * 2 + flip(core, part)
            if phase + part == 0:
                gradient = grad_p[0, 0, z, x]
            else:
                gradient = recv_y[phase, part, 0]
            gradient = gradient + recv_y[phase, part, 1]
            for xx in range(NX):
                g = gradient[4 * xx : 4 * xx + 4, :]
                old_master = state_recv[xx, owner, 0]
                old_moment = state_recv[xx, owner, 1]
                old_second = state_recv[xx, owner, 2]
                new_moment = 0.8 * old_moment + 0.2 * g
                new_second = 0.95 * old_second + 0.05 * g * g
                new_master = old_master - 0.3 * (new_moment / correct_one) / (
                    jnp.sqrt(new_second / correct_two) + 1e-08
                )
                result_send[xx, owner, 0] = new_master
                result_send[xx, owner, 1] = new_moment
                result_send[xx, owner, 2] = new_second
                rows_f32[4 * xx : 4 * xx + 4, :] = new_master
            rounded = rows_f32[...].astype(BF16)
            if phase == 0:
                own = gather_p.at[part, z, x, yl]
            else:
                own = gather_q.at[part, x, z, yl]
            own[...] = rounded
            gathered.append(send(own, own, y_peer(0, 0, 1)))

    result_recv[x] = result_send[x]

    def ring_gather(blocks, size, me, peer, half):
        long = 1 if half == 0 else -1
        lanes = [(long, size // 2), (-long, size // 2 - 1)]
        pending = {}
        for j in range(1, size // 2 + 1):
            for direction, steps in lanes:
                if j > steps:
                    continue
                if j > 1:
                    pending[direction].wait_recv()
                block = blocks.at[lax.rem(me - direction * (j - 1) + size, size)]
                pending[direction] = send(block, block, peer(direction))
            yield
        for message in pending.values():
            message.wait_recv()

    def gather(part, half):
        gathered[2 * part + half].wait_recv()
        if part == 0:
            blocks = gather_p.at[half]
            yield from ring_gather(blocks.at[z], NX, x, x_peer, half)
            yield from ring_gather(blocks, NZ, z, z_peer, half)
        else:
            blocks = gather_q.at[half]
            yield from ring_gather(blocks.at[x], NZ, z, z_peer, half)
            yield from ring_gather(blocks, NX, x, x_peer, half)

    tasks = [gather(part, half) for half in range(2) for part in range(2)]
    for task in tasks:
        next(task)
    result = []
    for k in (1, 2, 3):
        result.append(send(result_send.at[lax.rem(x + k, NX)], result_recv.at[x], x_peer(k)))
    run(tasks)

    for part in range(2):
        for half in range(2):
            owner = flip(yh, part) * 2 + flip(core, half)

            def place(zz, _):
                for xx in range(NX):
                    cols = pl.ds(pl.multiple_of(owner * 1024 + xx * 256, 256), 256)
                    for yy in range(NYL):
                        rows = pl.ds(pl.multiple_of(zz * 32 + yy * 16, 16), 16)
                        if part == 0:
                            out_weights[rows, cols] = gather_p[half, zz, xx, yy]
                        else:
                            out_weights[rows, cols] = gather_q[half, xx, zz, yy]
                return 0

            lax.fori_loop(0, NZ, place, 0)

    for message in result:
        message.wait_recv()
    for xx in range(NX):
        for w in range(4):
            cols = pl.ds(w * 1024 + xx * 256, 256)
            out_master[:, cols] = result_recv[xx, w, 0]
            out_moment[:, cols] = result_recv[xx, w, 1]
            out_second[:, cols] = result_recv[xx, w, 2]

    for message in messages:
        message.wait_send()


def per_device(left_factors, right_factors, fitness_rank, sign_index, master, moment, second):
    members = left_factors.shape[0]
    depth = members * R
    any_ = pl.BlockSpec(memory_space=pl.ANY)
    smem = pl.BlockSpec(memory_space=pltpu.SMEM)
    vmem = pl.BlockSpec(memory_space=pltpu.VMEM)
    return pl.pallas_call(
        kernel,
        out_shape=(
            jax.ShapeDtypeStruct(master.shape, F32),
            jax.ShapeDtypeStruct(master.shape, F32),
            jax.ShapeDtypeStruct(master.shape, F32),
            jax.ShapeDtypeStruct((256, 4096), BF16),
        ),
        in_specs=[any_, any_, smem, smem, any_, any_, any_],
        out_specs=(vmem, vmem, vmem, vmem),
        scratch_shapes=[
            pltpu.VMEM((4, depth, 256), BF16),
            pltpu.VMEM((4, depth, 256), BF16),
            pltpu.VMEM((NX, depth, 256), BF16),
            pltpu.VMEM((depth, 128), F32),
            pltpu.VMEM((3, 4, 4096), F32),
            pltpu.VMEM((2, 2, NZ, NX, 16, 256), F32),
            pltpu.VMEM((2, 2, NX, NZ, 16, 256), F32),
            pltpu.VMEM((2, 2, 7, NX, 16, 256), F32),
            pltpu.VMEM((2, 2, 3, 16, 256), F32),
            pltpu.VMEM((2, 2, 3, NZ, 16, 256), F32),
            pltpu.VMEM((2, 2, 7, 16, 256), F32),
            pltpu.VMEM((2, 2, 2, 16, 256), F32),
            pltpu.VMEM((NX, 4, 3, 4, 256), F32),
            pltpu.VMEM((NX, 4, 3, 4, 256), F32),
            pltpu.VMEM((NX, 4, 3, 4, 256), F32),
            pltpu.VMEM((NX, 4, 3, 4, 256), F32),
            pltpu.VMEM((16, 256), F32),
            pltpu.VMEM((2, NZ, NX, NYL, 16, 256), BF16),
            pltpu.VMEM((2, NX, NZ, NYL, 16, 256), BF16),
            pltpu.SemaphoreType.DMA((160,)),
            pltpu.SemaphoreType.DMA((160,)),
            pltpu.SemaphoreType.DMA((8,)),
        ],
        compiler_params=pltpu.CompilerParams(
            collective_id=0, has_side_effects=True, vmem_limit_bytes=48 << 20
        ),
    )(left_factors, right_factors, fitness_rank, sign_index, master, moment, second)


def solution(mesh):
    return jax.shard_map(
        per_device,
        mesh=mesh,
        in_specs=(
            P("pop", None, "wa"),
            P("pop", None, "wa"),
            P("pop"),
            P("pop"),
            P(("wa", "pop"), None),
            P(("wa", "pop"), None),
            P(("wa", "pop"), None),
        ),
        out_specs=(
            P(("wa", "pop"), None),
            P(("wa", "pop"), None),
            P(("wa", "pop"), None),
            P("wa", None),
        ),
        check_vma=False,
    )
```

```python
import math

import jax
import jax.numpy as jnp
from jax import lax
from jax.experimental import pallas as pl
from jax.experimental.pallas import tpu as pltpu
from jax.sharding import PartitionSpec as P

R = 4
STEP = 3
NZ, NYL, NX = 8, 2, 4
MESH = pl.DeviceIdType.MESH
F32 = jnp.float32
BF16 = jnp.bfloat16


def kernel(
    left_hbm, right_hbm, rank_hbm, sign_hbm, master_hbm, moment_hbm, second_hbm,
    out_master, out_moment, out_second, out_weights,
    rank_ref, sign_ref, left_raw, left_scaled, right, scale, adam_in,
    grad_p, grad_q, recv_p1, recv_p2, recv_q1, recv_q2, recv_y,
    state_send, state_recv, result_send, result_recv, rows_f32,
    gather_p, gather_q,
    send_sems, recv_sems, local_sems,
):
    members = rank_hbm.shape[0]
    depth = members * R
    pop = lax.axis_index("pop")
    wa = lax.axis_index("wa")
    z, yl, x = pop // (NYL * NX), lax.rem(pop // NX, NYL), lax.rem(pop, NX)
    yh, core = wa // 2, lax.rem(wa, 2)
    population = members * NZ * NYL * NX

    def flip(bit, by):
        return 1 - bit if by else bit

    def device(z_, yl_, x_, yh_, core_):
        return (z_ * (NYL * NX) + yl_ * NX + x_, yh_ * 2 + core_)

    def z_peer(step):
        return device(lax.rem(z + step + NZ, NZ), yl, x, yh, core)

    def x_peer(step):
        return device(z, yl, lax.rem(x + step + NX, NX), yh, core)

    def y_peer(phase, part, half):
        return device(z, flip(yl, half), x, flip(yh, phase), flip(core, part))

    others = [(a, b, c) for a in range(2) for b in range(2) for c in range(2) if a + b + c]
    plane = [(k, flip_y) for flip_y in range(2) for k in (2, 1, 3, 0) if k + flip_y]

    def plane_peer(k, flip_y):
        return device(z, flip(yl, flip_y), lax.rem(x + k, NX), yh, core)

    peers = [y_peer(*o) for o in others] + [z_peer(k) for k in range(1, NZ)]
    peers += [plane_peer(*o) for o in plane if o[0]]

    messages = []

    def send(src, dst, to):
        index = len(messages)
        message = pltpu.make_async_remote_copy(
            src_ref=src, dst_ref=dst, send_sem=send_sems.at[index],
            recv_sem=recv_sems.at[index], device_id=to, device_id_type=MESH,
        )
        message.start()
        messages.append(message)
        return message

    left_view = left_hbm.reshape(depth, left_hbm.shape[2])
    right_view = right_hbm.reshape(depth, right_hbm.shape[2])
    load_left = pltpu.make_async_copy(left_view, left_raw.at[0], local_sems.at[0])
    load_left.start()
    load_fitness = [
        pltpu.make_async_copy(rank_hbm, rank_ref, local_sems.at[8]),
        pltpu.make_async_copy(sign_hbm, sign_ref, local_sems.at[9]),
    ]
    load_right = []
    for c in range(NX):
        load_right.append(
            pltpu.make_async_copy(
                right_view.at[:, pl.ds(c * 256, 256)], right.at[c], local_sems.at[1 + c]
            )
        )
    load_state = [
        pltpu.make_async_copy(ref, adam_in.at[a], local_sems.at[5 + a])
        for a, ref in enumerate((master_hbm, moment_hbm, second_hbm))
    ]

    for copy in load_fitness + load_right + load_state:
        copy.start()

    barrier = pltpu.get_barrier_semaphore()
    for peer in peers:
        pl.semaphore_signal(barrier, inc=1, device_id=peer, device_id_type=MESH)
    pl.semaphore_wait(barrier, len(peers))

    to_chip = send(left_view, left_raw.at[2], y_peer(1, 0, 0))
    to_core = send(left_view, left_raw.at[1], y_peer(0, 1, 0))
    for copy in load_fitness:
        copy.wait()

    square_sum = population * (population + 1) / (3.0 * (population - 1))
    norm = 1.0 / ((population - 1) * math.sqrt(square_sum * R))
    upper = lax.broadcasted_iota(jnp.int32, (8, 128), 0) < R

    def fill(j, _):
        def centred(m):
            return (2 * rank_ref[m] - (population - 1)) * (1 - 2 * sign_ref[m])

        first, second_ = centred(2 * j), centred(2 * j + 1)
        both = jnp.where(upper, jnp.full((8, 128), first), jnp.full((8, 128), second_))
        scale[pl.ds(pl.multiple_of(8 * j, 8), 8), :] = both.astype(F32) * norm
        return 0

    lax.fori_loop(0, members // 2, fill, 0)

    def product(slot, phase, part):
        def scaling(k, _):
            rows = pl.ds(pl.multiple_of(k * 128, 128), 128)
            factor = scale[rows, :]
            for half in range(2):
                cols = pl.ds(half * 128, 128)
                left_scaled[slot, rows, cols] = (
                    left_raw[slot, rows, cols].astype(F32) * factor
                ).astype(BF16)
            return 0

        lax.fori_loop(0, depth // 128, scaling, 0)

        def columns(c, _):
            block = lax.dot_general(
                left_scaled[slot], right[c], (((0,), (0,)), ((), ())),
                preferred_element_type=F32,
            )
            for zz in range(NZ):
                for yy in range(NYL):
                    half = 1 - yl if yy else yl
                    at = zz * 32 + yy * 16
                    piece = block[at : at + 16, :]
                    if part == 0:
                        grad_p[phase, half, zz, c] = piece
                    else:
                        grad_q[phase, half, c, zz] = piece
            return 0

        lax.fori_loop(0, NX, columns, 0)

    def ring_sum(chunks, slots, first_slot, size, me, peer, half):
        long = 1 if half == 0 else -1
        lanes = []
        slot = first_slot
        for direction in (long, -long):
            steps = size // 2 if direction == long else size // 2 - 1
            lanes.append((direction, steps, slot))
            slot += steps
        pending = {}

        def chunk(direction, distance):
            return lax.rem(me + direction * distance + size, size)

        for direction, steps, slot in lanes:
            pending[direction] = send(
                chunks.at[chunk(direction, steps)], slots.at[slot], peer(direction)
            )
        yield
        for j in range(1, size // 2 + 1):
            for direction, steps, slot in lanes:
                if j > steps:
                    continue
                pending[direction].wait_recv()
                target = chunk(direction, steps - j)
                chunks[target] = chunks[target] + slots[slot + j - 1]
                if j < steps:
                    pending[direction] = send(
                        chunks.at[target], slots.at[slot + j], peer(direction)
                    )
            yield

    def direct_sum(chunks, slots, size, me, peer):
        sent = []
        for k in sorted(range(1, size), key=lambda k: -min(k, size - k)):
            sent.append(
                send(chunks.at[lax.rem(me + k, size)], slots.at[k - 1], peer(k))
            )
        yield
        for message in sent:
            message.wait_recv()
        total = chunks[me]
        for k in range(1, size):
            total = total + slots[k - 1]
        chunks[me] = total

    exchanged = {}

    def reduction(phase, part, half):
        if part == 0:
            own = grad_p.at[phase, half]
            yield from ring_sum(own, recv_p1.at[phase, half], 0, NZ, z, z_peer, half)
            own = own.at[z]
            yield from direct_sum(own, recv_p2.at[phase, half], NX, x, x_peer)
            own = own.at[x]
        else:
            own = grad_q.at[phase, half]
            yield from ring_sum(own, recv_q1.at[phase, half], 0, NX, x, x_peer, half)
            own = own.at[x]
            yield from direct_sum(own, recv_q2.at[phase, half], NZ, z, z_peer)
            own = own.at[z]
        if phase + part + half:
            exchanged[phase, part, half] = send(
                own, recv_y.at[phase, part, half], y_peer(phase, part, half)
            )

    def run(tasks, rounds=None):
        while tasks and rounds != 0:
            rounds = None if rounds is None else rounds - 1
            alive = []
            for task in tasks:
                try:
                    next(task)
                    alive.append(task)
                except StopIteration:
                    pass
            tasks = alive
        return tasks

    def begin(phase, part):
        tasks = [reduction(phase, part, half) for half in range(2)]
        for task in tasks:
            next(task)
        return tasks

    load_left.wait()
    for copy in load_right:
        copy.wait()
    product(0, 0, 0)
    tasks = begin(0, 0)
    to_core.wait_recv()
    product(1, 0, 1)
    tasks += begin(0, 1)

    for copy in load_state:
        copy.wait()
    for xx in range(NX):
        for w in range(4):
            for a in range(3):
                state_send[xx, w, a] = adam_in[a, :, pl.ds(w * 1024 + xx * 256, 256)]
    state_recv[x] = state_send[x]
    state = []
    for k in (1, 2, 3):
        state.append(send(state_send.at[lax.rem(x + k, NX)], state_recv.at[x], x_peer(k)))

    tasks = run(tasks, 5)
    to_chip.wait_recv()
    to_core2 = send(left_raw.at[2], left_raw.at[3], y_peer(0, 1, 0))
    product(2, 1, 0)
    later = begin(1, 0)
    run(tasks)
    to_core2.wait_recv()
    product(3, 1, 1)
    later += begin(1, 1)
    run(later)

    for message in state:
        message.wait_recv()
    for message in exchanged.values():
        message.wait_recv()
    correct_one = 1.0 - 0.8**STEP
    correct_two = 1.0 - 0.95**STEP
    gathered = []
    gathered_z = []
    for phase in range(2):
        for part in range(2):
            owner = flip(yh, phase) * 2 + flip(core, part)
            if phase + part == 0:
                gradient = grad_p[0, 0, z, x]
            else:
                gradient = recv_y[phase, part, 0]
            gradient = gradient + recv_y[phase, part, 1]
            for xx in range(NX):
                g = gradient[4 * xx : 4 * xx + 4, :]
                old_master = state_recv[xx, owner, 0]
                old_moment = state_recv[xx, owner, 1]
                old_second = state_recv[xx, owner, 2]
                new_moment = 0.8 * old_moment + 0.2 * g
                new_second = 0.95 * old_second + 0.05 * g * g
                new_master = old_master - 0.3 * (new_moment / correct_one) / (
                    jnp.sqrt(new_second / correct_two) + 1e-08
                )
                result_send[xx, owner, 0] = new_master
                result_send[xx, owner, 1] = new_moment
                result_send[xx, owner, 2] = new_second
                rows_f32[4 * xx : 4 * xx + 4, :] = new_master
            rounded = rows_f32[...].astype(BF16)
            if phase == 0:
                gather_p[z, x, yl, part] = rounded
            else:
                gather_q[x, yl, z, part] = rounded
        if phase == 0:
            own = gather_p.at[z, x, yl]
            for k, flip_y in plane:
                gathered.append(send(own, own, plane_peer(k, flip_y)))
        else:
            own = gather_q.at[x, yl, z]
            for k in (4, 3, 5, 2, 6, 1, 7):
                gathered_z.append(send(own, own, z_peer(k)))

    result_recv[x] = result_send[x]

    def ring_gather(half):
        long = 1 if half == 0 else -1
        lanes = [(long, NZ // 2), (-long, NZ // 2 - 1)]
        pending = {}
        for j in range(1, NZ // 2 + 1):
            for direction, steps in lanes:
                if j > steps:
                    continue
                if j > 1:
                    pending[direction].wait_recv()
                origin = lax.rem(z - direction * (j - 1) + NZ, NZ)
                block = gather_p.at[origin, pl.ds(2 * half, 2)]
                pending[direction] = send(block, block, z_peer(direction))
            yield
        for message in pending.values():
            message.wait_recv()

    for message in gathered:
        message.wait_recv()
    tasks = [ring_gather(half) for half in range(2)]
    for task in tasks:
        next(task)
    for message in gathered_z:
        message.wait_recv()
    own = gather_q.at[x, yl]
    gathered = [send(own, own, plane_peer(k, flip_y)) for k, flip_y in plane]
    result = []
    for k in (1, 2, 3):
        result.append(send(result_send.at[lax.rem(x + k, NX)], result_recv.at[x], x_peer(k)))
    run(tasks)
    for message in gathered:
        message.wait_recv()

    for part in range(2):
        for half in range(2):
            owner = flip(yh, part) * 2 + flip(core, half)

            def place(zz, _):
                for xx in range(NX):
                    cols = pl.ds(pl.multiple_of(owner * 1024 + xx * 256, 256), 256)
                    for yy in range(NYL):
                        rows = pl.ds(pl.multiple_of(zz * 32 + yy * 16, 16), 16)
                        if part == 0:
                            out_weights[rows, cols] = gather_p[zz, xx, yy, half]
                        else:
                            out_weights[rows, cols] = gather_q[xx, yy, zz, half]
                return 0

            lax.fori_loop(0, NZ, place, 0)

    for message in result:
        message.wait_recv()
    for xx in range(NX):
        for w in range(4):
            cols = pl.ds(w * 1024 + xx * 256, 256)
            out_master[:, cols] = result_recv[xx, w, 0]
            out_moment[:, cols] = result_recv[xx, w, 1]
            out_second[:, cols] = result_recv[xx, w, 2]

    for message in messages:
        message.wait_send()


def write_out(*refs):
    ins, outs, sems = refs[:4], refs[4:8], refs[8]
    copies = [pltpu.make_async_copy(ins[i], outs[i], sems.at[i]) for i in range(4)]
    for copy in reversed(copies):
        copy.start()
    for copy in copies:
        copy.wait()


def per_device(left_factors, right_factors, fitness_rank, sign_index, master, moment, second):
    members = left_factors.shape[0]
    depth = members * R
    hbm = pl.BlockSpec(memory_space=pltpu.HBM)
    any_ = pl.BlockSpec(memory_space=pl.ANY)
    vmem = pl.BlockSpec(memory_space=pltpu.VMEM)
    operands = [
        pltpu.with_memory_space_constraint(a, pltpu.HBM)
        for a in (left_factors, right_factors, fitness_rank, sign_index, master, moment, second)
    ]
    updated = pl.pallas_call(
        kernel,
        out_shape=(
            jax.ShapeDtypeStruct(master.shape, F32),
            jax.ShapeDtypeStruct(master.shape, F32),
            jax.ShapeDtypeStruct(master.shape, F32),
            jax.ShapeDtypeStruct((256, 4096), BF16),
        ),
        in_specs=[hbm] * 7,
        out_specs=(vmem, vmem, vmem, vmem),
        scratch_shapes=[
            pltpu.SMEM((members,), jnp.int32),
            pltpu.SMEM((members,), jnp.int32),
            pltpu.VMEM((4, depth, 256), BF16),
            pltpu.VMEM((4, depth, 256), BF16),
            pltpu.VMEM((NX, depth, 256), BF16),
            pltpu.VMEM((depth, 128), F32),
            pltpu.VMEM((3, 4, 4096), F32),
            pltpu.VMEM((2, 2, NZ, NX, 16, 256), F32),
            pltpu.VMEM((2, 2, NX, NZ, 16, 256), F32),
            pltpu.VMEM((2, 2, 7, NX, 16, 256), F32),
            pltpu.VMEM((2, 2, 3, 16, 256), F32),
            pltpu.VMEM((2, 2, 3, NZ, 16, 256), F32),
            pltpu.VMEM((2, 2, 7, 16, 256), F32),
            pltpu.VMEM((2, 2, 2, 16, 256), F32),
            pltpu.VMEM((NX, 4, 3, 4, 256), F32),
            pltpu.VMEM((NX, 4, 3, 4, 256), F32),
            pltpu.VMEM((NX, 4, 3, 4, 256), F32),
            pltpu.VMEM((NX, 4, 3, 4, 256), F32),
            pltpu.VMEM((16, 256), F32),
            pltpu.VMEM((NZ, NX, NYL, 2, 16, 256), BF16),
            pltpu.VMEM((NX, NYL, NZ, 2, 16, 256), BF16),
            pltpu.SemaphoreType.DMA((192,)),
            pltpu.SemaphoreType.DMA((192,)),
            pltpu.SemaphoreType.DMA((10,)),
        ],
        compiler_params=pltpu.CompilerParams(
            collective_id=0, has_side_effects=True, vmem_limit_bytes=48 << 20
        ),
    )(*operands)
    return pl.pallas_call(
        write_out,
        out_shape=tuple(jax.ShapeDtypeStruct(a.shape, a.dtype) for a in updated),
        in_specs=[any_] * 4,
        out_specs=(any_,) * 4,
        scratch_shapes=[pltpu.SemaphoreType.DMA((4,))],
    )(*updated)


def solution(mesh):
    return jax.shard_map(
        per_device,
        mesh=mesh,
        in_specs=(
            P("pop", None, "wa"),
            P("pop", None, "wa"),
            P("pop"),
            P("pop"),
            P(("wa", "pop"), None),
            P(("wa", "pop"), None),
            P(("wa", "pop"), None),
        ),
        out_specs=(
            P(("wa", "pop"), None),
            P(("wa", "pop"), None),
            P(("wa", "pop"), None),
            P("wa", None),
        ),
        check_vma=False,
    )
```

```python
import math

import jax
import jax.numpy as jnp
from jax import lax
from jax.experimental import pallas as pl
from jax.experimental.pallas import tpu as pltpu
from jax.sharding import PartitionSpec as P

R = 4
STEP = 3
NZ, NYL, NX = 8, 2, 4
MESH = pl.DeviceIdType.MESH
F32 = jnp.float32
BF16 = jnp.bfloat16


def kernel(
    left_hbm, right_hbm, rank_hbm, sign_hbm, master_hbm, moment_hbm, second_hbm,
    out_master, out_moment, out_second, out_weights,
    rank_ref, sign_ref, left_raw, left_scaled, right, scale, adam_in,
    grad_p, grad_q, recv_p1, recv_p2, recv_q1, recv_q2, recv_y,
    state_send, state_recv, result_send, result_recv, rows_f32,
    gather_p, gather_q,
    send_sems, recv_sems, local_sems,
):
    members = rank_hbm.shape[0]
    depth = members * R
    pop = lax.axis_index("pop")
    wa = lax.axis_index("wa")
    z, yl, x = pop // (NYL * NX), lax.rem(pop // NX, NYL), lax.rem(pop, NX)
    yh, core = wa // 2, lax.rem(wa, 2)
    population = members * NZ * NYL * NX

    def flip(bit, by):
        return 1 - bit if by else bit

    def device(z_, yl_, x_, yh_, core_):
        return (z_ * (NYL * NX) + yl_ * NX + x_, yh_ * 2 + core_)

    def z_peer(step):
        return device(lax.rem(z + step + NZ, NZ), yl, x, yh, core)

    def x_peer(step):
        return device(z, yl, lax.rem(x + step + NX, NX), yh, core)

    def y_peer(phase, part, half):
        return device(z, flip(yl, half), x, flip(yh, phase), flip(core, part))

    others = [(a, b, c) for a in range(2) for b in range(2) for c in range(2) if a + b + c]
    plane = [(k, flip_y) for flip_y in range(2) for k in (2, 1, 3, 0) if k + flip_y]

    def plane_peer(k, flip_y):
        return device(z, flip(yl, flip_y), lax.rem(x + k, NX), yh, core)

    peers = [y_peer(*o) for o in others] + [z_peer(k) for k in range(1, NZ)]
    peers += [plane_peer(*o) for o in plane if o[0]]

    messages = []

    def send(src, dst, to):
        index = len(messages)
        message = pltpu.make_async_remote_copy(
            src_ref=src, dst_ref=dst, send_sem=send_sems.at[index],
            recv_sem=recv_sems.at[index], device_id=to, device_id_type=MESH,
        )
        message.start()
        messages.append(message)
        return message

    left_view = left_hbm.reshape(depth, left_hbm.shape[2])
    right_view = right_hbm.reshape(depth, right_hbm.shape[2])
    load_left = pltpu.make_async_copy(left_view, left_raw.at[0], local_sems.at[0])
    load_left.start()
    load_fitness = [
        pltpu.make_async_copy(rank_hbm, rank_ref, local_sems.at[8]),
        pltpu.make_async_copy(sign_hbm, sign_ref, local_sems.at[9]),
    ]
    load_right = []
    for c in range(NX):
        load_right.append(
            pltpu.make_async_copy(
                right_view.at[:, pl.ds(c * 256, 256)], right.at[c], local_sems.at[1 + c]
            )
        )
    load_state = [
        pltpu.make_async_copy(ref, adam_in.at[a], local_sems.at[5 + a])
        for a, ref in enumerate((master_hbm, moment_hbm, second_hbm))
    ]

    for copy in load_fitness + load_right + load_state:
        copy.start()

    barrier = pltpu.get_barrier_semaphore()
    for peer in peers:
        pl.semaphore_signal(barrier, inc=1, device_id=peer, device_id_type=MESH)
    pl.semaphore_wait(barrier, len(peers))

    halves = [pl.ds(0, depth // 2), pl.ds(depth // 2, depth // 2)]
    to_chip = [
        send(left_view.at[rows], left_raw.at[2, rows], y_peer(1, 0, 0)) for rows in halves
    ]
    to_core = send(left_view, left_raw.at[1], y_peer(0, 1, 0))
    for copy in load_fitness:
        copy.wait()

    square_sum = population * (population + 1) / (3.0 * (population - 1))
    norm = 1.0 / ((population - 1) * math.sqrt(square_sum * R))
    upper = lax.broadcasted_iota(jnp.int32, (8, 128), 0) < R

    def fill(j, _):
        def centred(m):
            return (2 * rank_ref[m] - (population - 1)) * (1 - 2 * sign_ref[m])

        first, second_ = centred(2 * j), centred(2 * j + 1)
        both = jnp.where(upper, jnp.full((8, 128), first), jnp.full((8, 128), second_))
        scale[pl.ds(pl.multiple_of(8 * j, 8), 8), :] = both.astype(F32) * norm
        return 0

    lax.fori_loop(0, members // 2, fill, 0)

    def product(slot, phase, part):
        def scaling(k, _):
            rows = pl.ds(pl.multiple_of(k * 128, 128), 128)
            factor = scale[rows, :]
            for half in range(2):
                cols = pl.ds(half * 128, 128)
                left_scaled[slot, rows, cols] = (
                    left_raw[slot, rows, cols].astype(F32) * factor
                ).astype(BF16)
            return 0

        lax.fori_loop(0, depth // 128, scaling, 0)

        def columns(c, _):
            block = lax.dot_general(
                left_scaled[slot], right[c], (((0,), (0,)), ((), ())),
                preferred_element_type=F32,
            )
            for zz in range(NZ):
                for yy in range(NYL):
                    half = 1 - yl if yy else yl
                    at = zz * 32 + yy * 16
                    piece = block[at : at + 16, :]
                    if part == phase:
                        grad_p[phase, half, zz, c] = piece
                    else:
                        grad_q[phase, half, c, zz] = piece
            return 0

        lax.fori_loop(0, NX, columns, 0)

    def ring_sum(chunks, slots, first_slot, size, me, peer, half):
        long = 1 if half == 0 else -1
        lanes = []
        slot = first_slot
        for direction in (long, -long):
            steps = size // 2 if direction == long else size // 2 - 1
            lanes.append((direction, steps, slot))
            slot += steps
        pending = {}

        def chunk(direction, distance):
            return lax.rem(me + direction * distance + size, size)

        for direction, steps, slot in lanes:
            pending[direction] = send(
                chunks.at[chunk(direction, steps)], slots.at[slot], peer(direction)
            )
        yield
        for j in range(1, size // 2 + 1):
            for direction, steps, slot in lanes:
                if j > steps:
                    continue
                pending[direction].wait_recv()
                target = chunk(direction, steps - j)
                chunks[target] = chunks[target] + slots[slot + j - 1]
                if j < steps:
                    pending[direction] = send(
                        chunks.at[target], slots.at[slot + j], peer(direction)
                    )
            if j < size // 2:
                yield

    def direct_sum(chunks, slots, size, me, peer):
        sent = []
        for k in sorted(range(1, size), key=lambda k: -min(k, size - k)):
            sent.append(
                send(chunks.at[lax.rem(me + k, size)], slots.at[k - 1], peer(k))
            )
        yield
        for message in sent:
            message.wait_recv()
        total = chunks[me]
        for k in range(1, size):
            total = total + slots[k - 1]
        chunks[me] = total

    exchanged = {}

    def reduction(phase, part, half):
        if part == phase:
            own = grad_p.at[phase, half]
            yield from ring_sum(own, recv_p1.at[phase, half], 0, NZ, z, z_peer, half)
            own = own.at[z]
            yield from direct_sum(own, recv_p2.at[phase, half], NX, x, x_peer)
            own = own.at[x]
        else:
            own = grad_q.at[phase, half]
            yield from ring_sum(own, recv_q1.at[phase, half], 0, NX, x, x_peer, half)
            own = own.at[x]
            yield from direct_sum(own, recv_q2.at[phase, half], NZ, z, z_peer)
            own = own.at[z]
        if phase + part + half:
            exchanged[phase, part, half] = send(
                own, recv_y.at[phase, part, half], y_peer(phase, part, half)
            )

    def step(tasks):
        for task in tasks:
            next(task, None)

    def begin(phase, part):
        tasks = [reduction(phase, part, half) for half in range(2)]
        step(tasks)
        return tasks

    load_left.wait()
    for copy in load_right:
        copy.wait()
    product(0, 0, 0)
    p0 = begin(0, 0)
    to_core.wait_recv()
    product(1, 0, 1)
    q0 = begin(0, 1)

    for copy in load_state:
        copy.wait()
    for xx in range(NX):
        for w in range(4):
            for a in range(3):
                state_send[xx, w, a] = adam_in[a, :, pl.ds(w * 1024 + xx * 256, 256)]
    state_recv[x] = state_send[x]
    state = []
    for k in (1, 2, 3):
        state.append(send(state_send.at[lax.rem(x + k, NX)], state_recv.at[x], x_peer(k)))

    for tasks in (p0, q0, p0, q0, p0, p0):
        step(tasks)
    to_core2 = []
    for message, rows in zip(to_chip, halves):
        message.wait_recv()
        to_core2.append(
            send(left_raw.at[2, rows], left_raw.at[3, rows], y_peer(0, 1, 0))
        )
    product(2, 1, 0)
    q1 = begin(1, 0)
    step(q0)
    step(p0)
    for message in to_core2:
        message.wait_recv()
    product(3, 1, 1)
    p1 = begin(1, 1)

    for message in state:
        message.wait_recv()
    correct_one = 1.0 - 0.8**STEP
    correct_two = 1.0 - 0.95**STEP

    def update(phase):
        for part in range(2):
            owner = flip(yh, phase) * 2 + flip(core, part)
            for half in range(2):
                if phase + part + half:
                    exchanged[phase, part, half].wait_recv()
            if phase + part == 0:
                gradient = grad_p[0, 0, z, x]
            else:
                gradient = recv_y[phase, part, 0]
            gradient = gradient + recv_y[phase, part, 1]
            for xx in range(NX):
                g = gradient[4 * xx : 4 * xx + 4, :]
                old_master = state_recv[xx, owner, 0]
                old_moment = state_recv[xx, owner, 1]
                old_second = state_recv[xx, owner, 2]
                new_moment = 0.8 * old_moment + 0.2 * g
                new_second = 0.95 * old_second + 0.05 * g * g
                new_master = old_master - 0.3 * (new_moment / correct_one) / (
                    jnp.sqrt(new_second / correct_two) + 1e-08
                )
                result_send[xx, owner, 0] = new_master
                result_send[xx, owner, 1] = new_moment
                result_send[xx, owner, 2] = new_second
                rows_f32[4 * xx : 4 * xx + 4, :] = new_master
            rounded = rows_f32[...].astype(BF16)
            if phase == 0:
                gather_p[z, x, yl, part] = rounded
            else:
                gather_q[x, yl, z, part] = rounded

    def ring_gather(half):
        long = 1 if half == 0 else -1
        lanes = [(long, NZ // 2), (-long, NZ // 2 - 1)]
        pending = {}
        for j in range(1, NZ // 2 + 1):
            for direction, steps in lanes:
                if j > steps:
                    continue
                if j > 1:
                    pending[direction].wait_recv()
                origin = lax.rem(z - direction * (j - 1) + NZ, NZ)
                block = gather_p.at[origin, pl.ds(2 * half, 2)]
                pending[direction] = send(block, block, z_peer(direction))
            yield
        for message in pending.values():
            message.wait_recv()

    def ring_p():
        update(0)
        own = gather_p.at[z, x, yl]
        sent = [send(own, own, plane_peer(k, flip_y)) for k, flip_y in plane]
        yield
        for message in sent:
            message.wait_recv()
        tasks = [ring_gather(half) for half in range(2)]
        for _ in range(NZ // 2):
            step(tasks)
            yield
        step(tasks)

    gather0 = [ring_p()]
    for tasks in (gather0, q1, p1, gather0, p1, q1, gather0, p1, gather0, p1, q1, gather0, p1):
        step(tasks)
    update(1)
    own = gather_q.at[x, yl, z]
    sent = [send(own, own, z_peer(k)) for k in (4, 3, 5, 2, 6, 1, 7)]
    result = []
    for k in (1, 2, 3):
        result.append(send(result_send.at[lax.rem(x + k, NX)], result_recv.at[x], x_peer(k)))
    result_recv[x] = result_send[x]
    for message in sent:
        message.wait_recv()
    own = gather_q.at[x, yl]
    gathered = [send(own, own, plane_peer(k, flip_y)) for k, flip_y in plane]
    step(gather0)

    for part in range(2):
        if part == 1:
            for message in gathered:
                message.wait_recv()
        for half in range(2):
            owner = flip(yh, part) * 2 + flip(core, half)

            def place(zz, _):
                for xx in range(NX):
                    cols = pl.ds(pl.multiple_of(owner * 1024 + xx * 256, 256), 256)
                    for yy in range(NYL):
                        rows = pl.ds(pl.multiple_of(zz * 32 + yy * 16, 16), 16)
                        if part == 0:
                            out_weights[rows, cols] = gather_p[zz, xx, yy, half]
                        else:
                            out_weights[rows, cols] = gather_q[xx, yy, zz, half]
                return 0

            lax.fori_loop(0, NZ, place, 0)

    for message in result:
        message.wait_recv()
    for xx in range(NX):
        for w in range(4):
            cols = pl.ds(w * 1024 + xx * 256, 256)
            out_master[:, cols] = result_recv[xx, w, 0]
            out_moment[:, cols] = result_recv[xx, w, 1]
            out_second[:, cols] = result_recv[xx, w, 2]

    for message in messages:
        message.wait_send()


def write_out(*refs):
    ins, outs, sems = refs[:4], refs[4:8], refs[8]
    copies = [pltpu.make_async_copy(ins[i], outs[i], sems.at[i]) for i in range(4)]
    for copy in reversed(copies):
        copy.start()
    for copy in copies:
        copy.wait()


def per_device(left_factors, right_factors, fitness_rank, sign_index, master, moment, second):
    members = left_factors.shape[0]
    depth = members * R
    hbm = pl.BlockSpec(memory_space=pltpu.HBM)
    any_ = pl.BlockSpec(memory_space=pl.ANY)
    vmem = pl.BlockSpec(memory_space=pltpu.VMEM)
    operands = [
        pltpu.with_memory_space_constraint(a, pltpu.HBM)
        for a in (left_factors, right_factors, fitness_rank, sign_index, master, moment, second)
    ]
    updated = pl.pallas_call(
        kernel,
        out_shape=(
            jax.ShapeDtypeStruct(master.shape, F32),
            jax.ShapeDtypeStruct(master.shape, F32),
            jax.ShapeDtypeStruct(master.shape, F32),
            jax.ShapeDtypeStruct((256, 4096), BF16),
        ),
        in_specs=[hbm] * 7,
        out_specs=(vmem, vmem, vmem, vmem),
        scratch_shapes=[
            pltpu.SMEM((members,), jnp.int32),
            pltpu.SMEM((members,), jnp.int32),
            pltpu.VMEM((4, depth, 256), BF16),
            pltpu.VMEM((4, depth, 256), BF16),
            pltpu.VMEM((NX, depth, 256), BF16),
            pltpu.VMEM((depth, 128), F32),
            pltpu.VMEM((3, 4, 4096), F32),
            pltpu.VMEM((2, 2, NZ, NX, 16, 256), F32),
            pltpu.VMEM((2, 2, NX, NZ, 16, 256), F32),
            pltpu.VMEM((2, 2, 7, NX, 16, 256), F32),
            pltpu.VMEM((2, 2, 3, 16, 256), F32),
            pltpu.VMEM((2, 2, 3, NZ, 16, 256), F32),
            pltpu.VMEM((2, 2, 7, 16, 256), F32),
            pltpu.VMEM((2, 2, 2, 16, 256), F32),
            pltpu.VMEM((NX, 4, 3, 4, 256), F32),
            pltpu.VMEM((NX, 4, 3, 4, 256), F32),
            pltpu.VMEM((NX, 4, 3, 4, 256), F32),
            pltpu.VMEM((NX, 4, 3, 4, 256), F32),
            pltpu.VMEM((16, 256), F32),
            pltpu.VMEM((NZ, NX, NYL, 2, 16, 256), BF16),
            pltpu.VMEM((NX, NYL, NZ, 2, 16, 256), BF16),
            pltpu.SemaphoreType.DMA((192,)),
            pltpu.SemaphoreType.DMA((192,)),
            pltpu.SemaphoreType.DMA((10,)),
        ],
        compiler_params=pltpu.CompilerParams(
            collective_id=0, has_side_effects=True, vmem_limit_bytes=48 << 20
        ),
    )(*operands)
    return pl.pallas_call(
        write_out,
        out_shape=tuple(jax.ShapeDtypeStruct(a.shape, a.dtype) for a in updated),
        in_specs=[any_] * 4,
        out_specs=(any_,) * 4,
        scratch_shapes=[pltpu.SemaphoreType.DMA((4,))],
        compiler_params=pltpu.CompilerParams(vmem_limit_bytes=1 << 20),
    )(*updated)


def solution(mesh):
    return jax.shard_map(
        per_device,
        mesh=mesh,
        in_specs=(
            P("pop", None, "wa"),
            P("pop", None, "wa"),
            P("pop"),
            P("pop"),
            P(("wa", "pop"), None),
            P(("wa", "pop"), None),
            P(("wa", "pop"), None),
        ),
        out_specs=(
            P(("wa", "pop"), None),
            P(("wa", "pop"), None),
            P(("wa", "pop"), None),
            P("wa", None),
        ),
        check_vma=False,
    )
```

```python
import math

import jax
import jax.numpy as jnp
from jax import lax
from jax.experimental import pallas as pl
from jax.experimental.pallas import tpu as pltpu
from jax.sharding import PartitionSpec as P

R = 4
STEP = 3
NZ, NYL, NX = 8, 2, 4
PLACE = [0, 1, 7, 2, 6, 3, 5, 4]
MESH = pl.DeviceIdType.MESH
F32 = jnp.float32
BF16 = jnp.bfloat16


def kernel(
    left_hbm, right_hbm, rank_hbm, sign_hbm, master_hbm, moment_hbm, second_hbm,
    out_master, out_moment, out_second, out_weights,
    rank_ref, sign_ref, left_raw, left_scaled, right, scale, adam_in,
    grad_p, grad_q, recv_p1, recv_p2, recv_q1, recv_q2, recv_y,
    state_send, state_recv, result_send, result_recv, rows_f32,
    gather_p, gather_q,
    send_sems, recv_sems, local_sems,
):
    members = rank_hbm.shape[0]
    depth = members * R
    pop = lax.axis_index("pop")
    wa = lax.axis_index("wa")
    z, yl, x = pop // (NYL * NX), lax.rem(pop // NX, NYL), lax.rem(pop, NX)
    yh, core = wa // 2, lax.rem(wa, 2)
    population = members * NZ * NYL * NX

    def flip(bit, by):
        return 1 - bit if by else bit

    def device(z_, yl_, x_, yh_, core_):
        return (z_ * (NYL * NX) + yl_ * NX + x_, yh_ * 2 + core_)

    def z_peer(step):
        return device(lax.rem(z + step + NZ, NZ), yl, x, yh, core)

    def x_peer(step):
        return device(z, yl, lax.rem(x + step + NX, NX), yh, core)

    def y_peer(phase, part, half):
        return device(z, flip(yl, half), x, flip(yh, phase), flip(core, part))

    others = [(a, b, c) for a in range(2) for b in range(2) for c in range(2) if a + b + c]
    plane = [(k, flip_y) for flip_y in range(2) for k in (2, 1, 3, 0) if k + flip_y]

    def plane_peer(k, flip_y):
        return device(z, flip(yl, flip_y), lax.rem(x + k, NX), yh, core)

    peers = [y_peer(*o) for o in others] + [z_peer(k) for k in range(1, NZ)]
    peers += [plane_peer(*o) for o in plane if o[0]]

    messages = []

    def send(src, dst, to):
        index = len(messages)
        message = pltpu.make_async_remote_copy(
            src_ref=src, dst_ref=dst, send_sem=send_sems.at[index],
            recv_sem=recv_sems.at[index], device_id=to, device_id_type=MESH,
        )
        message.start()
        messages.append(message)
        return message

    left_view = left_hbm.reshape(depth, left_hbm.shape[2])
    right_view = right_hbm.reshape(depth, right_hbm.shape[2])
    load_left = pltpu.make_async_copy(left_view, left_raw.at[0], local_sems.at[0])
    load_left.start()
    load_fitness = [
        pltpu.make_async_copy(rank_hbm, rank_ref, local_sems.at[8]),
        pltpu.make_async_copy(sign_hbm, sign_ref, local_sems.at[9]),
    ]
    load_right = []
    for c in range(NX):
        load_right.append(
            pltpu.make_async_copy(
                right_view.at[:, pl.ds(c * 256, 256)], right.at[c], local_sems.at[1 + c]
            )
        )
    load_state = [
        pltpu.make_async_copy(ref, adam_in.at[a], local_sems.at[5 + a])
        for a, ref in enumerate((master_hbm, moment_hbm, second_hbm))
    ]

    for copy in load_fitness + load_right + load_state:
        copy.start()

    barrier = pltpu.get_barrier_semaphore()
    for peer in peers:
        pl.semaphore_signal(barrier, inc=1, device_id=peer, device_id_type=MESH)
    pl.semaphore_wait(barrier, len(peers))

    halves = [pl.ds(0, depth // 2), pl.ds(depth // 2, depth // 2)]
    to_chip = [
        send(left_view.at[rows], left_raw.at[2, rows], y_peer(1, 0, 0)) for rows in halves
    ]
    to_core = send(left_view, left_raw.at[1], y_peer(0, 1, 0))
    for copy in load_fitness:
        copy.wait()

    square_sum = population * (population + 1) / (3.0 * (population - 1))
    norm = 1.0 / ((population - 1) * math.sqrt(square_sum * R))
    upper = lax.broadcasted_iota(jnp.int32, (8, 128), 0) < R

    def fill(j, _):
        def centred(m):
            return (2 * rank_ref[m] - (population - 1)) * (1 - 2 * sign_ref[m])

        first, second_ = centred(2 * j), centred(2 * j + 1)
        both = jnp.where(upper, jnp.full((8, 128), first), jnp.full((8, 128), second_))
        scale[pl.ds(pl.multiple_of(8 * j, 8), 8), :] = both.astype(F32) * norm
        return 0

    lax.fori_loop(0, members // 2, fill, 0)

    def product(slot, phase, part):
        def scaling(k, _):
            rows = pl.ds(pl.multiple_of(k * 128, 128), 128)
            factor = scale[rows, :]
            for half in range(2):
                cols = pl.ds(half * 128, 128)
                left_scaled[slot, rows, cols] = (
                    left_raw[slot, rows, cols].astype(F32) * factor
                ).astype(BF16)
            return 0

        lax.fori_loop(0, depth // 128, scaling, 0)

        def columns(c, _):
            block = lax.dot_general(
                left_scaled[slot], right[c], (((0,), (0,)), ((), ())),
                preferred_element_type=F32,
            )
            for zz in range(NZ):
                for yy in range(NYL):
                    half = 1 - yl if yy else yl
                    at = zz * 32 + yy * 16
                    piece = block[at : at + 16, :]
                    if part == phase:
                        grad_p[phase, half, zz, c] = piece
                    else:
                        grad_q[phase, half, c, zz] = piece
            return 0

        lax.fori_loop(0, NX, columns, 0)

    def ring_sum(chunks, slots, first_slot, size, me, peer, half):
        long = 1 if half == 0 else -1
        lanes = []
        slot = first_slot
        for direction in (long, -long):
            steps = size // 2 if direction == long else size // 2 - 1
            lanes.append((direction, steps, slot))
            slot += steps
        pending = {}

        def chunk(direction, distance):
            return lax.rem(me + direction * distance + size, size)

        for direction, steps, slot in lanes:
            pending[direction] = send(
                chunks.at[chunk(direction, steps)], slots.at[slot], peer(direction)
            )
        yield
        for j in range(1, size // 2 + 1):
            for direction, steps, slot in lanes:
                if j > steps:
                    continue
                pending[direction].wait_recv()
                target = chunk(direction, steps - j)
                chunks[target] = chunks[target] + slots[slot + j - 1]
                if j < steps:
                    pending[direction] = send(
                        chunks.at[target], slots.at[slot + j], peer(direction)
                    )
            if j < size // 2:
                yield

    def direct_sum(chunks, slots, size, me, peer):
        sent = []
        for k in sorted(range(1, size), key=lambda k: -min(k, size - k)):
            sent.append(
                send(chunks.at[lax.rem(me + k, size)], slots.at[k - 1], peer(k))
            )
        yield
        for message in sent:
            message.wait_recv()
        total = chunks[me]
        for k in range(1, size):
            total = total + slots[k - 1]
        chunks[me] = total

    exchanged = {}

    def reduction(phase, part, half):
        if part == phase:
            own = grad_p.at[phase, half]
            yield from ring_sum(own, recv_p1.at[phase, half], 0, NZ, z, z_peer, half)
            own = own.at[z]
            yield from direct_sum(own, recv_p2.at[phase, half], NX, x, x_peer)
            own = own.at[x]
        else:
            own = grad_q.at[phase, half]
            yield from ring_sum(own, recv_q1.at[phase, half], 0, NX, x, x_peer, half)
            own = own.at[x]
            yield from direct_sum(own, recv_q2.at[phase, half], NZ, z, z_peer)
            own = own.at[z]
        if phase + part + half:
            exchanged[phase, part, half] = send(
                own, recv_y.at[phase, part, half], y_peer(phase, part, half)
            )

    def step(tasks):
        for task in tasks:
            next(task, None)

    def begin(phase, part):
        tasks = [reduction(phase, part, half) for half in range(2)]
        step(tasks)
        return tasks

    load_left.wait()
    for copy in load_right:
        copy.wait()
    product(0, 0, 0)
    p0 = begin(0, 0)
    to_core.wait_recv()
    product(1, 0, 1)
    q0 = begin(0, 1)

    for copy in load_state:
        copy.wait()
    for xx in range(NX):
        for w in range(4):
            for a in range(3):
                state_send[xx, w, a] = adam_in[a, :, pl.ds(w * 1024 + xx * 256, 256)]
    state_recv[x] = state_send[x]
    state = []
    for k in (1, 2, 3):
        state.append(send(state_send.at[lax.rem(x + k, NX)], state_recv.at[x], x_peer(k)))

    for tasks in (p0, q0, p0, q0, p0):
        step(tasks)
    to_core2 = []
    for message, rows in zip(to_chip, halves):
        message.wait_recv()
        to_core2.append(
            send(left_raw.at[2, rows], left_raw.at[3, rows], y_peer(0, 1, 0))
        )
    product(2, 1, 0)
    q1 = begin(1, 0)
    step(p0)
    for message in to_core2:
        message.wait_recv()
    product(3, 1, 1)
    p1 = begin(1, 1)

    for message in state:
        message.wait_recv()
    correct_one = 1.0 - 0.8**STEP
    correct_two = 1.0 - 0.95**STEP

    blocks = (gather_p, gather_q)
    columns_sent = ({}, {})
    result = []

    def return_results(phase):
        for k in (1, 2, 3):
            to = result_recv.at[phase, x]
            result.append(send(result_send.at[phase, lax.rem(x + k, NX)], to, x_peer(k)))
        result_recv[phase, x] = result_send[phase, x]

    def update(phase):
        for part in range(2):
            owner = flip(yh, phase) * 2 + flip(core, part)
            for half in range(2):
                if phase + part + half:
                    exchanged[phase, part, half].wait_recv()
            if phase + part == 0:
                gradient = grad_p[0, 0, z, x]
            else:
                gradient = recv_y[phase, part, 0]
            gradient = gradient + recv_y[phase, part, 1]
            for xx in range(NX):
                g = gradient[4 * xx : 4 * xx + 4, :]
                old_master = state_recv[xx, owner, 0]
                old_moment = state_recv[xx, owner, 1]
                old_second = state_recv[xx, owner, 2]
                new_moment = 0.8 * old_moment + 0.2 * g
                new_second = 0.95 * old_second + 0.05 * g * g
                new_master = old_master - 0.3 * (new_moment / correct_one) / (
                    jnp.sqrt(new_second / correct_two) + 1e-08
                )
                result_send[phase, xx, part, 0] = new_master
                result_send[phase, xx, part, 1] = new_moment
                result_send[phase, xx, part, 2] = new_second
                rows_f32[4 * xx : 4 * xx + 4, :] = new_master
            rounded = rows_f32[...].astype(BF16)
            blocks[phase][x, yl, 0, part] = rounded
        for k in (4, 3, 5, 2, 6, 1, 7):
            own = blocks[phase].at[x, yl, 0]
            to = blocks[phase].at[x, yl, PLACE.index(NZ - k)]
            columns_sent[phase][NZ - k] = send(own, to, z_peer(k))

    def spread(phase, first, count):
        for distance in PLACE[first : first + count]:
            if distance:
                columns_sent[phase][distance].wait_recv()
        own = blocks[phase].at[x, yl, pl.ds(first, count)]
        return [send(own, own, plane_peer(k, flip_y)) for k, flip_y in plane]

    def place(phase):
        for part in range(2):
            owner = flip(yh, phase) * 2 + flip(core, part)
            for distance in range(NZ):
                first_row = lax.rem(z + distance, NZ) * 32

                def put(xx, _):
                    cols = pl.ds(pl.multiple_of(owner * 1024 + xx * 256, 256), 256)
                    for yy in range(NYL):
                        rows = pl.ds(pl.multiple_of(first_row + yy * 16, 16), 16)
                        block = blocks[phase][xx, yy, PLACE.index(distance), part]
                        out_weights[rows, cols] = block
                    return 0

                lax.fori_loop(0, NX, put, 0)

    def gather0():
        update(0)
        yield
        gathered.extend(spread(0, 0, NZ))
        return_results(0)

    gathered = []
    g0 = [gather0()]
    for tasks in (q0, p0, q1, p1, g0, q1, p1, g0, p1, p1, q1, p1):
        step(tasks)
    update(1)
    last = spread(1, 0, 1)
    last += spread(1, 1, 4)
    last += spread(1, 5, 3)
    return_results(1)
    for message in gathered:
        message.wait_recv()
    place(0)
    for message in last:
        message.wait_recv()
    place(1)

    for message in result:
        message.wait_recv()
    for xx in range(NX):
        for phase in range(2):
            for part in range(2):
                owner = flip(yh, phase) * 2 + flip(core, part)
                cols = pl.ds(pl.multiple_of(owner * 1024 + xx * 256, 256), 256)
                out_master[:, cols] = result_recv[phase, xx, part, 0]
                out_moment[:, cols] = result_recv[phase, xx, part, 1]
                out_second[:, cols] = result_recv[phase, xx, part, 2]

    for message in messages:
        message.wait_send()


def write_out(*refs):
    ins, outs, sems = refs[:4], refs[4:8], refs[8]
    copies = [pltpu.make_async_copy(ins[i], outs[i], sems.at[i]) for i in range(4)]
    for copy in reversed(copies):
        copy.start()
    for copy in copies:
        copy.wait()


def per_device(left_factors, right_factors, fitness_rank, sign_index, master, moment, second):
    members = left_factors.shape[0]
    depth = members * R
    hbm = pl.BlockSpec(memory_space=pltpu.HBM)
    any_ = pl.BlockSpec(memory_space=pl.ANY)
    vmem = pl.BlockSpec(memory_space=pltpu.VMEM)
    operands = [
        pltpu.with_memory_space_constraint(a, pltpu.HBM)
        for a in (left_factors, right_factors, fitness_rank, sign_index, master, moment, second)
    ]
    updated = pl.pallas_call(
        kernel,
        out_shape=(
            jax.ShapeDtypeStruct(master.shape, F32),
            jax.ShapeDtypeStruct(master.shape, F32),
            jax.ShapeDtypeStruct(master.shape, F32),
            jax.ShapeDtypeStruct((256, 4096), BF16),
        ),
        in_specs=[hbm] * 7,
        out_specs=(vmem, vmem, vmem, vmem),
        scratch_shapes=[
            pltpu.SMEM((members,), jnp.int32),
            pltpu.SMEM((members,), jnp.int32),
            pltpu.VMEM((4, depth, 256), BF16),
            pltpu.VMEM((4, depth, 256), BF16),
            pltpu.VMEM((NX, depth, 256), BF16),
            pltpu.VMEM((depth, 128), F32),
            pltpu.VMEM((3, 4, 4096), F32),
            pltpu.VMEM((2, 2, NZ, NX, 16, 256), F32),
            pltpu.VMEM((2, 2, NX, NZ, 16, 256), F32),
            pltpu.VMEM((2, 2, 7, NX, 16, 256), F32),
            pltpu.VMEM((2, 2, 3, 16, 256), F32),
            pltpu.VMEM((2, 2, 3, NZ, 16, 256), F32),
            pltpu.VMEM((2, 2, 7, 16, 256), F32),
            pltpu.VMEM((2, 2, 2, 16, 256), F32),
            pltpu.VMEM((NX, 4, 3, 4, 256), F32),
            pltpu.VMEM((NX, 4, 3, 4, 256), F32),
            pltpu.VMEM((2, NX, 2, 3, 4, 256), F32),
            pltpu.VMEM((2, NX, 2, 3, 4, 256), F32),
            pltpu.VMEM((16, 256), F32),
            pltpu.VMEM((NX, NYL, NZ, 2, 16, 256), BF16),
            pltpu.VMEM((NX, NYL, NZ, 2, 16, 256), BF16),
            pltpu.SemaphoreType.DMA((192,)),
            pltpu.SemaphoreType.DMA((192,)),
            pltpu.SemaphoreType.DMA((10,)),
        ],
        compiler_params=pltpu.CompilerParams(
            collective_id=0, has_side_effects=True, vmem_limit_bytes=48 << 20
        ),
    )(*operands)
    return pl.pallas_call(
        write_out,
        out_shape=tuple(jax.ShapeDtypeStruct(a.shape, a.dtype) for a in updated),
        in_specs=[any_] * 4,
        out_specs=(any_,) * 4,
        scratch_shapes=[pltpu.SemaphoreType.DMA((4,))],
        compiler_params=pltpu.CompilerParams(vmem_limit_bytes=1 << 20),
    )(*updated)


def solution(mesh):
    return jax.shard_map(
        per_device,
        mesh=mesh,
        in_specs=(
            P("pop", None, "wa"),
            P("pop", None, "wa"),
            P("pop"),
            P("pop"),
            P(("wa", "pop"), None),
            P(("wa", "pop"), None),
            P(("wa", "pop"), None),
        ),
        out_specs=(
            P(("wa", "pop"), None),
            P(("wa", "pop"), None),
            P(("wa", "pop"), None),
            P("wa", None),
        ),
        check_vma=False,
    )
```

```python
import math

import jax
import jax.numpy as jnp
from jax import lax
from jax.experimental import pallas as pl
from jax.experimental.pallas import tpu as pltpu
from jax.sharding import PartitionSpec as P

R = 4
STEP = 3
NZ, NYL, NX = 8, 2, 4
PLACE = [0, 1, 7, 2, 6, 3, 5, 4]
MESH = pl.DeviceIdType.MESH
F32 = jnp.float32
BF16 = jnp.bfloat16


def kernel(
    left_hbm, right_hbm, rank_hbm, sign_hbm, master_hbm, moment_hbm, second_hbm,
    out_master, out_moment, out_second, out_weights,
    rank_ref, sign_ref, left_raw, left_scaled, right, scale, adam_in,
    grad_p, grad_q, recv_p1, recv_p2, recv_q1, recv_q2, recv_y,
    state_send, state_recv, result_send, result_recv, rows_f32,
    gather_p, gather_q,
    send_sems, recv_sems, local_sems,
):
    members = rank_hbm.shape[0]
    depth = members * R
    pop = lax.axis_index("pop")
    wa = lax.axis_index("wa")
    z, yl, x = pop // (NYL * NX), lax.rem(pop // NX, NYL), lax.rem(pop, NX)
    yh, core = wa // 2, lax.rem(wa, 2)
    population = members * NZ * NYL * NX

    def flip(bit, by):
        return 1 - bit if by else bit

    def device(z_, yl_, x_, yh_, core_):
        return (z_ * (NYL * NX) + yl_ * NX + x_, yh_ * 2 + core_)

    def z_peer(step):
        return device(lax.rem(z + step + NZ, NZ), yl, x, yh, core)

    def x_peer(step):
        return device(z, yl, lax.rem(x + step + NX, NX), yh, core)

    def y_peer(phase, part, half):
        return device(z, flip(yl, half), x, flip(yh, phase), flip(core, part))

    others = [(a, b, c) for a in range(2) for b in range(2) for c in range(2) if a + b + c]
    plane = [(k, flip_y) for flip_y in range(2) for k in (2, 1, 3, 0) if k + flip_y]

    def plane_peer(k, flip_y):
        return device(z, flip(yl, flip_y), lax.rem(x + k, NX), yh, core)

    peers = [y_peer(*o) for o in others] + [z_peer(k) for k in range(1, NZ)]
    peers += [plane_peer(*o) for o in plane if o[0]]

    messages = []

    def send(src, dst, to):
        index = len(messages)
        message = pltpu.make_async_remote_copy(
            src_ref=src, dst_ref=dst, send_sem=send_sems.at[index],
            recv_sem=recv_sems.at[index], device_id=to, device_id_type=MESH,
        )
        message.start()
        messages.append(message)
        return message

    left_view = left_hbm.reshape(depth, left_hbm.shape[2])
    right_view = right_hbm.reshape(depth, right_hbm.shape[2])
    load_left = pltpu.make_async_copy(left_view, left_raw.at[0], local_sems.at[0])
    load_left.start()
    load_fitness = [
        pltpu.make_async_copy(rank_hbm, rank_ref, local_sems.at[8]),
        pltpu.make_async_copy(sign_hbm, sign_ref, local_sems.at[9]),
    ]
    load_right = []
    for c in range(NX):
        load_right.append(
            pltpu.make_async_copy(
                right_view.at[:, pl.ds(c * 256, 256)], right.at[c], local_sems.at[1 + c]
            )
        )
    load_state = [
        pltpu.make_async_copy(ref, adam_in.at[a], local_sems.at[5 + a])
        for a, ref in enumerate((master_hbm, moment_hbm, second_hbm))
    ]

    for copy in load_fitness + load_right + load_state:
        copy.start()

    barrier = pltpu.get_barrier_semaphore()
    for peer in peers:
        pl.semaphore_signal(barrier, inc=1, device_id=peer, device_id_type=MESH)
    pl.semaphore_wait(barrier, len(peers))

    halves = [pl.ds(0, depth // 2), pl.ds(depth // 2, depth // 2)]
    to_chip = [
        send(left_view.at[rows], left_raw.at[2, rows], y_peer(1, 0, 0)) for rows in halves
    ]
    to_core = send(left_view, left_raw.at[1], y_peer(0, 1, 0))
    for copy in load_fitness:
        copy.wait()

    square_sum = population * (population + 1) / (3.0 * (population - 1))
    norm = 1.0 / ((population - 1) * math.sqrt(square_sum * R))
    upper = lax.broadcasted_iota(jnp.int32, (8, 128), 0) < R

    def fill(j, _):
        def centred(m):
            return (2 * rank_ref[m] - (population - 1)) * (1 - 2 * sign_ref[m])

        first, second_ = centred(2 * j), centred(2 * j + 1)
        both = jnp.where(upper, jnp.full((8, 128), first), jnp.full((8, 128), second_))
        scale[pl.ds(pl.multiple_of(8 * j, 8), 8), :] = both.astype(F32) * norm
        return 0

    lax.fori_loop(0, members // 2, fill, 0)

    def product(slot, phase, part):
        def scaling(k, _):
            rows = pl.ds(pl.multiple_of(k * 128, 128), 128)
            factor = scale[rows, :]
            for half in range(2):
                cols = pl.ds(half * 128, 128)
                left_scaled[slot, rows, cols] = (
                    left_raw[slot, rows, cols].astype(F32) * factor
                ).astype(BF16)
            return 0

        lax.fori_loop(0, depth // 128, scaling, 0)

        def columns(c, _):
            block = lax.dot_general(
                left_scaled[slot], right[c], (((0,), (0,)), ((), ())),
                preferred_element_type=F32,
            )
            for zz in range(NZ):
                for yy in range(NYL):
                    half = 1 - yl if yy else yl
                    at = zz * 32 + yy * 16
                    piece = block[at : at + 16, :]
                    if part == phase:
                        grad_p[phase, half, zz, c] = piece
                    else:
                        grad_q[phase, half, c, zz] = piece
            return 0

        lax.fori_loop(0, NX, columns, 0)

    def ring_sum(chunks, slots, first_slot, size, me, peer, half):
        long = 1 if half == 0 else -1
        lanes = []
        slot = first_slot
        for direction in (long, -long):
            steps = size // 2 if direction == long else size // 2 - 1
            lanes.append((direction, steps, slot))
            slot += steps
        pending = {}

        def chunk(direction, distance):
            return lax.rem(me + direction * distance + size, size)

        for direction, steps, slot in lanes:
            pending[direction] = send(
                chunks.at[chunk(direction, steps)], slots.at[slot], peer(direction)
            )
        yield
        for j in range(1, size // 2 + 1):
            for direction, steps, slot in lanes:
                if j > steps:
                    continue
                pending[direction].wait_recv()
                target = chunk(direction, steps - j)
                chunks[target] = chunks[target] + slots[slot + j - 1]
                if j < steps:
                    pending[direction] = send(
                        chunks.at[target], slots.at[slot + j], peer(direction)
                    )
            if j < size // 2:
                yield

    def direct_sum(chunks, slots, size, me, peer):
        sent = []
        for k in sorted(range(1, size), key=lambda k: -min(k, size - k)):
            sent.append(
                send(chunks.at[lax.rem(me + k, size)], slots.at[k - 1], peer(k))
            )
        yield
        for message in sent:
            message.wait_recv()
        total = chunks[me]
        for k in range(1, size):
            total = total + slots[k - 1]
        chunks[me] = total

    exchanged = {}

    def reduction(phase, part, half):
        if part == phase:
            own = grad_p.at[phase, half]
            yield from ring_sum(own, recv_p1.at[phase, half], 0, NZ, z, z_peer, half)
            own = own.at[z]
            yield from direct_sum(own, recv_p2.at[phase, half], NX, x, x_peer)
            own = own.at[x]
        else:
            own = grad_q.at[phase, half]
            yield from ring_sum(own, recv_q1.at[phase, half], 0, NX, x, x_peer, half)
            own = own.at[x]
            yield from direct_sum(own, recv_q2.at[phase, half], NZ, z, z_peer)
            own = own.at[z]
        if phase + part + half:
            exchanged[phase, part, half] = send(
                own, recv_y.at[phase, part, half], y_peer(phase, part, half)
            )

    def step(tasks):
        for task in tasks:
            next(task, None)

    def begin(phase, part):
        tasks = [reduction(phase, part, half) for half in range(2)]
        step(tasks)
        return tasks

    load_left.wait()
    for copy in load_right:
        copy.wait()
    product(0, 0, 0)
    p0 = begin(0, 0)
    to_core.wait_recv()
    product(1, 0, 1)
    q0 = begin(0, 1)

    for copy in load_state:
        copy.wait()
    for xx in range(NX):
        for w in range(4):
            for a in range(3):
                state_send[xx, w, a] = adam_in[a, :, pl.ds(w * 1024 + xx * 256, 256)]
    state_recv[x] = state_send[x]
    state = []
    for k in (1, 2, 3):
        state.append(send(state_send.at[lax.rem(x + k, NX)], state_recv.at[x], x_peer(k)))

    for tasks in (p0, q0, p0, q0):
        step(tasks)
    to_core2 = []
    for message, rows in zip(to_chip, halves):
        message.wait_recv()
        to_core2.append(
            send(left_raw.at[2, rows], left_raw.at[3, rows], y_peer(0, 1, 0))
        )
    product(2, 1, 0)
    q1 = begin(1, 0)
    step(p0)
    for message in to_core2:
        message.wait_recv()
    product(3, 1, 1)
    p1 = begin(1, 1)

    for message in state:
        message.wait_recv()
    correct_one = 1.0 - 0.8**STEP
    correct_two = 1.0 - 0.95**STEP

    blocks = (gather_p, gather_q)
    columns_sent = ({}, {})
    result = []

    def return_results(phase):
        for k in (1, 2, 3):
            to = result_recv.at[phase, x]
            result.append(send(result_send.at[phase, lax.rem(x + k, NX)], to, x_peer(k)))
        result_recv[phase, x] = result_send[phase, x]

    def update(phase):
        for part in range(2):
            owner = flip(yh, phase) * 2 + flip(core, part)
            for half in range(2):
                if phase + part + half:
                    exchanged[phase, part, half].wait_recv()
            if phase + part == 0:
                gradient = grad_p[0, 0, z, x]
            else:
                gradient = recv_y[phase, part, 0]
            gradient = gradient + recv_y[phase, part, 1]
            for xx in range(NX):
                g = gradient[4 * xx : 4 * xx + 4, :]
                old_master = state_recv[xx, owner, 0]
                old_moment = state_recv[xx, owner, 1]
                old_second = state_recv[xx, owner, 2]
                new_moment = 0.8 * old_moment + 0.2 * g
                new_second = 0.95 * old_second + 0.05 * g * g
                new_master = old_master - 0.3 * (new_moment / correct_one) / (
                    jnp.sqrt(new_second / correct_two) + 1e-08
                )
                result_send[phase, xx, part, 0] = new_master
                result_send[phase, xx, part, 1] = new_moment
                result_send[phase, xx, part, 2] = new_second
                rows_f32[4 * xx : 4 * xx + 4, :] = new_master
            rounded = rows_f32[...].astype(BF16)
            blocks[phase][x, yl, 0, part] = rounded
        for k in (4, 3, 5, 2, 6, 1, 7):
            own = blocks[phase].at[x, yl, 0]
            to = blocks[phase].at[x, yl, PLACE.index(NZ - k)]
            columns_sent[phase][NZ - k] = send(own, to, z_peer(k))

    def spread(phase, first, count):
        for distance in PLACE[first : first + count]:
            if distance:
                columns_sent[phase][distance].wait_recv()
        own = blocks[phase].at[x, yl, pl.ds(first, count)]
        return [send(own, own, plane_peer(k, flip_y)) for k, flip_y in plane]

    def place(phase):
        for part in range(2):
            owner = flip(yh, phase) * 2 + flip(core, part)
            for distance in range(NZ):
                first_row = lax.rem(z + distance, NZ) * 32

                def put(xx, _):
                    cols = pl.ds(pl.multiple_of(owner * 1024 + xx * 256, 256), 256)
                    for yy in range(NYL):
                        rows = pl.ds(pl.multiple_of(first_row + yy * 16, 16), 16)
                        block = blocks[phase][xx, yy, PLACE.index(distance), part]
                        out_weights[rows, cols] = block
                    return 0

                lax.fori_loop(0, NX, put, 0)

    def gather0():
        update(0)
        yield
        gathered.extend(spread(0, 0, NZ))
        return_results(0)

    gathered = []
    g0 = [gather0()]
    for tasks in (p0, q0, p0, p1, q1, g0, p1, q1, g0, p1, p1, q1, p1):
        step(tasks)
    update(1)
    last = spread(1, 0, 1)
    last += spread(1, 1, 2)
    last += spread(1, 3, 5)
    return_results(1)
    for message in gathered:
        message.wait_recv()
    place(0)
    for message in last:
        message.wait_recv()
    place(1)

    for message in result:
        message.wait_recv()
    for xx in range(NX):
        for phase in range(2):
            for part in range(2):
                owner = flip(yh, phase) * 2 + flip(core, part)
                cols = pl.ds(pl.multiple_of(owner * 1024 + xx * 256, 256), 256)
                out_master[:, cols] = result_recv[phase, xx, part, 0]
                out_moment[:, cols] = result_recv[phase, xx, part, 1]
                out_second[:, cols] = result_recv[phase, xx, part, 2]

    for message in messages:
        message.wait_send()


def write_out(*refs):
    ins, outs, sems = refs[:4], refs[4:8], refs[8]
    copies = [pltpu.make_async_copy(ins[i], outs[i], sems.at[i]) for i in range(4)]
    for copy in reversed(copies):
        copy.start()
    for copy in copies:
        copy.wait()


def per_device(left_factors, right_factors, fitness_rank, sign_index, master, moment, second):
    members = left_factors.shape[0]
    depth = members * R
    hbm = pl.BlockSpec(memory_space=pltpu.HBM)
    any_ = pl.BlockSpec(memory_space=pl.ANY)
    vmem = pl.BlockSpec(memory_space=pltpu.VMEM)
    operands = [
        pltpu.with_memory_space_constraint(a, pltpu.HBM)
        for a in (left_factors, right_factors, fitness_rank, sign_index, master, moment, second)
    ]
    updated = pl.pallas_call(
        kernel,
        out_shape=(
            jax.ShapeDtypeStruct(master.shape, F32),
            jax.ShapeDtypeStruct(master.shape, F32),
            jax.ShapeDtypeStruct(master.shape, F32),
            jax.ShapeDtypeStruct((256, 4096), BF16),
        ),
        in_specs=[hbm] * 7,
        out_specs=(vmem, vmem, vmem, vmem),
        scratch_shapes=[
            pltpu.SMEM((members,), jnp.int32),
            pltpu.SMEM((members,), jnp.int32),
            pltpu.VMEM((4, depth, 256), BF16),
            pltpu.VMEM((4, depth, 256), BF16),
            pltpu.VMEM((NX, depth, 256), BF16),
            pltpu.VMEM((depth, 128), F32),
            pltpu.VMEM((3, 4, 4096), F32),
            pltpu.VMEM((2, 2, NZ, NX, 16, 256), F32),
            pltpu.VMEM((2, 2, NX, NZ, 16, 256), F32),
            pltpu.VMEM((2, 2, 7, NX, 16, 256), F32),
            pltpu.VMEM((2, 2, 3, 16, 256), F32),
            pltpu.VMEM((2, 2, 3, NZ, 16, 256), F32),
            pltpu.VMEM((2, 2, 7, 16, 256), F32),
            pltpu.VMEM((2, 2, 2, 16, 256), F32),
            pltpu.VMEM((NX, 4, 3, 4, 256), F32),
            pltpu.VMEM((NX, 4, 3, 4, 256), F32),
            pltpu.VMEM((2, NX, 2, 3, 4, 256), F32),
            pltpu.VMEM((2, NX, 2, 3, 4, 256), F32),
            pltpu.VMEM((16, 256), F32),
            pltpu.VMEM((NX, NYL, NZ, 2, 16, 256), BF16),
            pltpu.VMEM((NX, NYL, NZ, 2, 16, 256), BF16),
            pltpu.SemaphoreType.DMA((192,)),
            pltpu.SemaphoreType.DMA((192,)),
            pltpu.SemaphoreType.DMA((10,)),
        ],
        compiler_params=pltpu.CompilerParams(
            collective_id=0, has_side_effects=True, vmem_limit_bytes=48 << 20
        ),
    )(*operands)
    return pl.pallas_call(
        write_out,
        out_shape=tuple(jax.ShapeDtypeStruct(a.shape, a.dtype) for a in updated),
        in_specs=[any_] * 4,
        out_specs=(any_,) * 4,
        scratch_shapes=[pltpu.SemaphoreType.DMA((4,))],
        compiler_params=pltpu.CompilerParams(vmem_limit_bytes=1 << 20),
    )(*updated)


def solution(mesh):
    return jax.shard_map(
        per_device,
        mesh=mesh,
        in_specs=(
            P("pop", None, "wa"),
            P("pop", None, "wa"),
            P("pop"),
            P("pop"),
            P(("wa", "pop"), None),
            P(("wa", "pop"), None),
            P(("wa", "pop"), None),
        ),
        out_specs=(
            P(("wa", "pop"), None),
            P(("wa", "pop"), None),
            P(("wa", "pop"), None),
            P("wa", None),
        ),
        check_vma=False,
    )
```

```python
import math

import jax
import jax.numpy as jnp
from jax import lax
from jax.experimental import pallas as pl
from jax.experimental.pallas import tpu as pltpu
from jax.sharding import PartitionSpec as P

R = 4
STEP = 3
NZ, NYL, NX = 8, 2, 4
PLACE = [0, 1, 7, 2, 6, 3, 5, 4]
MESH = pl.DeviceIdType.MESH
F32 = jnp.float32
BF16 = jnp.bfloat16


def kernel(
    left_hbm, right_hbm, rank_hbm, sign_hbm, master_hbm, moment_hbm, second_hbm,
    out_master, out_moment, out_second, out_weights,
    rank_ref, sign_ref, left_raw, left_scaled, right, scale, adam_in,
    grad_p, grad_q, recv_p1, recv_p2, recv_q1, recv_q2, recv_y,
    state_send, state_recv, result_send, result_recv, rows_f32,
    gather_p, gather_q,
    send_sems, recv_sems, local_sems,
):
    members = rank_hbm.shape[0]
    depth = members * R
    pop = lax.axis_index("pop")
    wa = lax.axis_index("wa")
    z, yl, x = pop // (NYL * NX), lax.rem(pop // NX, NYL), lax.rem(pop, NX)
    yh, core = wa // 2, lax.rem(wa, 2)
    population = members * NZ * NYL * NX

    def flip(bit, by):
        return 1 - bit if by else bit

    def device(z_, yl_, x_, yh_, core_):
        return (z_ * (NYL * NX) + yl_ * NX + x_, yh_ * 2 + core_)

    def z_peer(step):
        return device(lax.rem(z + step + NZ, NZ), yl, x, yh, core)

    def x_peer(step):
        return device(z, yl, lax.rem(x + step + NX, NX), yh, core)

    def y_peer(phase, part, half):
        return device(z, flip(yl, half), x, flip(yh, phase), flip(core, part))

    others = [(a, b, c) for a in range(2) for b in range(2) for c in range(2) if a + b + c]
    plane = [(k, flip_y) for flip_y in range(2) for k in (2, 1, 3, 0) if k + flip_y]

    def plane_peer(k, flip_y):
        return device(z, flip(yl, flip_y), lax.rem(x + k, NX), yh, core)

    peers = [y_peer(*o) for o in others] + [z_peer(k) for k in range(1, NZ)]
    peers += [plane_peer(*o) for o in plane if o[0]]

    messages = []

    def send(src, dst, to):
        index = len(messages)
        message = pltpu.make_async_remote_copy(
            src_ref=src, dst_ref=dst, send_sem=send_sems.at[index],
            recv_sem=recv_sems.at[index], device_id=to, device_id_type=MESH,
        )
        message.start()
        messages.append(message)
        return message

    left_view = left_hbm.reshape(depth, left_hbm.shape[2])
    right_view = right_hbm.reshape(depth, right_hbm.shape[2])
    load_left = pltpu.make_async_copy(left_view, left_raw.at[0], local_sems.at[0])
    load_left.start()
    load_fitness = [
        pltpu.make_async_copy(rank_hbm, rank_ref, local_sems.at[8]),
        pltpu.make_async_copy(sign_hbm, sign_ref, local_sems.at[9]),
    ]
    load_right = []
    for c in range(NX):
        load_right.append(
            pltpu.make_async_copy(
                right_view.at[:, pl.ds(c * 256, 256)], right.at[c], local_sems.at[1 + c]
            )
        )
    load_state = [
        pltpu.make_async_copy(ref, adam_in.at[a], local_sems.at[5 + a])
        for a, ref in enumerate((master_hbm, moment_hbm, second_hbm))
    ]

    for copy in load_fitness + load_right + load_state:
        copy.start()

    barrier = pltpu.get_barrier_semaphore()
    for peer in peers:
        pl.semaphore_signal(barrier, inc=1, device_id=peer, device_id_type=MESH)
    pl.semaphore_wait(barrier, len(peers))

    halves = [pl.ds(0, depth // 2), pl.ds(depth // 2, depth // 2)]
    to_chip = [
        send(left_view.at[rows], left_raw.at[2, rows], y_peer(1, 0, 0)) for rows in halves
    ]
    to_core = send(left_view, left_raw.at[1], y_peer(0, 1, 0))
    for copy in load_fitness:
        copy.wait()

    square_sum = population * (population + 1) / (3.0 * (population - 1))
    norm = 1.0 / ((population - 1) * math.sqrt(square_sum * R))
    upper = lax.broadcasted_iota(jnp.int32, (8, 128), 0) < R

    def fill(j, _):
        def centred(m):
            return (2 * rank_ref[m] - (population - 1)) * (1 - 2 * sign_ref[m])

        first, second_ = centred(2 * j), centred(2 * j + 1)
        both = jnp.where(upper, jnp.full((8, 128), first), jnp.full((8, 128), second_))
        scale[pl.ds(pl.multiple_of(8 * j, 8), 8), :] = both.astype(F32) * norm
        return 0

    lax.fori_loop(0, members // 2, fill, 0)

    def product(slot, phase, part):
        def scaling(k, _):
            rows = pl.ds(pl.multiple_of(k * 128, 128), 128)
            factor = scale[rows, :]
            for half in range(2):
                cols = pl.ds(half * 128, 128)
                left_scaled[slot, rows, cols] = (
                    left_raw[slot, rows, cols].astype(F32) * factor
                ).astype(BF16)
            return 0

        lax.fori_loop(0, depth // 128, scaling, 0, unroll=4)

        def columns(c, _):
            block = lax.dot_general(
                left_scaled[slot], right[c], (((0,), (0,)), ((), ())),
                preferred_element_type=F32,
            )
            for zz in range(NZ):
                for yy in range(NYL):
                    half = 1 - yl if yy else yl
                    at = zz * 32 + yy * 16
                    piece = block[at : at + 16, :]
                    if part == phase:
                        grad_p[phase, half, zz, c] = piece
                    else:
                        grad_q[phase, half, c, zz] = piece
            return 0

        lax.fori_loop(0, NX, columns, 0, unroll=True)

    def ring_sum(chunks, slots, first_slot, size, me, peer, half):
        long = 1 if half == 0 else -1
        lanes = []
        slot = first_slot
        for direction in (long, -long):
            steps = size // 2 if direction == long else size // 2 - 1
            lanes.append((direction, steps, slot))
            slot += steps
        pending = {}

        def chunk(direction, distance):
            return lax.rem(me + direction * distance + size, size)

        for direction, steps, slot in lanes:
            pending[direction] = send(
                chunks.at[chunk(direction, steps)], slots.at[slot], peer(direction)
            )
        yield
        for j in range(1, size // 2 + 1):
            for direction, steps, slot in lanes:
                if j > steps:
                    continue
                pending[direction].wait_recv()
                target = chunk(direction, steps - j)
                chunks[target] = chunks[target] + slots[slot + j - 1]
                if j < steps:
                    pending[direction] = send(
                        chunks.at[target], slots.at[slot + j], peer(direction)
                    )
            if j < size // 2:
                yield

    def direct_sum(chunks, slots, size, me, peer):
        sent = []
        for k in sorted(range(1, size), key=lambda k: -min(k, size - k)):
            sent.append(
                send(chunks.at[lax.rem(me + k, size)], slots.at[k - 1], peer(k))
            )
        yield
        for message in sent:
            message.wait_recv()
        total = chunks[me]
        for k in range(1, size):
            total = total + slots[k - 1]
        chunks[me] = total

    exchanged = {}

    def reduction(phase, part, half):
        if part == phase:
            own = grad_p.at[phase, half]
            yield from ring_sum(own, recv_p1.at[phase, half], 0, NZ, z, z_peer, half)
            own = own.at[z]
            yield from direct_sum(own, recv_p2.at[phase, half], NX, x, x_peer)
            own = own.at[x]
        else:
            own = grad_q.at[phase, half]
            yield from ring_sum(own, recv_q1.at[phase, half], 0, NX, x, x_peer, half)
            own = own.at[x]
            yield from direct_sum(own, recv_q2.at[phase, half], NZ, z, z_peer)
            own = own.at[z]
        if phase + part + half:
            exchanged[phase, part, half] = send(
                own, recv_y.at[phase, part, half], y_peer(phase, part, half)
            )

    def step(tasks):
        for task in tasks:
            next(task, None)

    def begin(phase, part):
        tasks = [reduction(phase, part, half) for half in range(2)]
        step(tasks)
        return tasks

    load_left.wait()
    for copy in load_right:
        copy.wait()
    product(0, 0, 0)
    p0 = begin(0, 0)
    to_core.wait_recv()
    product(1, 0, 1)
    q0 = begin(0, 1)

    for copy in load_state:
        copy.wait()
    for xx in range(NX):
        for w in range(4):
            for a in range(3):
                state_send[xx, w, a] = adam_in[a, :, pl.ds(w * 1024 + xx * 256, 256)]
    state_recv[x] = state_send[x]
    state = []
    for k in (1, 2, 3):
        state.append(send(state_send.at[lax.rem(x + k, NX)], state_recv.at[x], x_peer(k)))

    for tasks in (p0, q0, p0, q0):
        step(tasks)
    to_core2 = []
    for message, rows in zip(to_chip, halves):
        message.wait_recv()
        to_core2.append(
            send(left_raw.at[2, rows], left_raw.at[3, rows], y_peer(0, 1, 0))
        )
    product(2, 1, 0)
    q1 = begin(1, 0)
    step(p0)
    for message in to_core2:
        message.wait_recv()
    product(3, 1, 1)
    p1 = begin(1, 1)

    for message in state:
        message.wait_recv()
    correct_one = 1.0 - 0.8**STEP
    correct_two = 1.0 - 0.95**STEP

    blocks = (gather_p, gather_q)
    columns_sent = ({}, {})
    result = []

    def return_results(phase):
        for k in (1, 2, 3):
            to = result_recv.at[phase, x]
            result.append(send(result_send.at[phase, lax.rem(x + k, NX)], to, x_peer(k)))
        result_recv[phase, x] = result_send[phase, x]

    def update(phase):
        for part in range(2):
            owner = flip(yh, phase) * 2 + flip(core, part)
            for half in range(2):
                if phase + part + half:
                    exchanged[phase, part, half].wait_recv()
            if phase + part == 0:
                gradient = grad_p[0, 0, z, x]
            else:
                gradient = recv_y[phase, part, 0]
            gradient = gradient + recv_y[phase, part, 1]
            for xx in range(NX):
                g = gradient[4 * xx : 4 * xx + 4, :]
                old_master = state_recv[xx, owner, 0]
                old_moment = state_recv[xx, owner, 1]
                old_second = state_recv[xx, owner, 2]
                new_moment = 0.8 * old_moment + 0.2 * g
                new_second = 0.95 * old_second + 0.05 * g * g
                new_master = old_master - 0.3 * (new_moment / correct_one) / (
                    jnp.sqrt(new_second / correct_two) + 1e-08
                )
                result_send[phase, xx, part, 0] = new_master
                result_send[phase, xx, part, 1] = new_moment
                result_send[phase, xx, part, 2] = new_second
                rows_f32[4 * xx : 4 * xx + 4, :] = new_master
            rounded = rows_f32[...].astype(BF16)
            blocks[phase][x, yl, 0, part] = rounded
        for k in (4, 3, 5, 2, 6, 1, 7):
            own = blocks[phase].at[x, yl, 0]
            to = blocks[phase].at[x, yl, PLACE.index(NZ - k)]
            columns_sent[phase][NZ - k] = send(own, to, z_peer(k))

    def spread(phase, first, count):
        for distance in PLACE[first : first + count]:
            if distance:
                columns_sent[phase][distance].wait_recv()
        own = blocks[phase].at[x, yl, pl.ds(first, count)]
        return [send(own, own, plane_peer(k, flip_y)) for k, flip_y in plane]

    def place(phase):
        for part in range(2):
            owner = flip(yh, phase) * 2 + flip(core, part)
            for distance in range(NZ):
                first_row = lax.rem(z + distance, NZ) * 32

                def put(xx, _):
                    cols = pl.ds(pl.multiple_of(owner * 1024 + xx * 256, 256), 256)
                    for yy in range(NYL):
                        rows = pl.ds(pl.multiple_of(first_row + yy * 16, 16), 16)
                        block = blocks[phase][xx, yy, PLACE.index(distance), part]
                        out_weights[rows, cols] = block
                    return 0

                lax.fori_loop(0, NX, put, 0)

    def gather0():
        update(0)
        yield
        gathered.extend(spread(0, 0, NZ))
        return_results(0)

    gathered = []
    g0 = [gather0()]
    for tasks in (p0, q0, p0, p1, q1, g0, p1, q1, g0, p1, p1, q1, p1):
        step(tasks)
    update(1)
    last = spread(1, 0, 1)
    last += spread(1, 1, 2)
    last += spread(1, 3, 5)
    return_results(1)
    for message in gathered:
        message.wait_recv()
    place(0)
    for message in last:
        message.wait_recv()
    place(1)

    for message in result:
        message.wait_recv()
    for xx in range(NX):
        for phase in range(2):
            for part in range(2):
                owner = flip(yh, phase) * 2 + flip(core, part)
                cols = pl.ds(pl.multiple_of(owner * 1024 + xx * 256, 256), 256)
                out_master[:, cols] = result_recv[phase, xx, part, 0]
                out_moment[:, cols] = result_recv[phase, xx, part, 1]
                out_second[:, cols] = result_recv[phase, xx, part, 2]

    for message in messages:
        message.wait_send()


def write_out(*refs):
    ins, outs, sems = refs[:4], refs[4:8], refs[8]
    copies = [pltpu.make_async_copy(ins[i], outs[i], sems.at[i]) for i in range(4)]
    for copy in reversed(copies):
        copy.start()
    for copy in copies:
        copy.wait()


def per_device(left_factors, right_factors, fitness_rank, sign_index, master, moment, second):
    members = left_factors.shape[0]
    depth = members * R
    hbm = pl.BlockSpec(memory_space=pltpu.HBM)
    any_ = pl.BlockSpec(memory_space=pl.ANY)
    vmem = pl.BlockSpec(memory_space=pltpu.VMEM)
    operands = [
        pltpu.with_memory_space_constraint(a, pltpu.HBM)
        for a in (left_factors, right_factors, fitness_rank, sign_index, master, moment, second)
    ]
    updated = pl.pallas_call(
        kernel,
        out_shape=(
            jax.ShapeDtypeStruct(master.shape, F32),
            jax.ShapeDtypeStruct(master.shape, F32),
            jax.ShapeDtypeStruct(master.shape, F32),
            jax.ShapeDtypeStruct((256, 4096), BF16),
        ),
        in_specs=[hbm] * 7,
        out_specs=(vmem, vmem, vmem, vmem),
        scratch_shapes=[
            pltpu.SMEM((members,), jnp.int32),
            pltpu.SMEM((members,), jnp.int32),
            pltpu.VMEM((4, depth, 256), BF16),
            pltpu.VMEM((4, depth, 256), BF16),
            pltpu.VMEM((NX, depth, 256), BF16),
            pltpu.VMEM((depth, 128), F32),
            pltpu.VMEM((3, 4, 4096), F32),
            pltpu.VMEM((2, 2, NZ, NX, 16, 256), F32),
            pltpu.VMEM((2, 2, NX, NZ, 16, 256), F32),
            pltpu.VMEM((2, 2, 7, NX, 16, 256), F32),
            pltpu.VMEM((2, 2, 3, 16, 256), F32),
            pltpu.VMEM((2, 2, 3, NZ, 16, 256), F32),
            pltpu.VMEM((2, 2, 7, 16, 256), F32),
            pltpu.VMEM((2, 2, 2, 16, 256), F32),
            pltpu.VMEM((NX, 4, 3, 4, 256), F32),
            pltpu.VMEM((NX, 4, 3, 4, 256), F32),
            pltpu.VMEM((2, NX, 2, 3, 4, 256), F32),
            pltpu.VMEM((2, NX, 2, 3, 4, 256), F32),
            pltpu.VMEM((16, 256), F32),
            pltpu.VMEM((NX, NYL, NZ, 2, 16, 256), BF16),
            pltpu.VMEM((NX, NYL, NZ, 2, 16, 256), BF16),
            pltpu.SemaphoreType.DMA((192,)),
            pltpu.SemaphoreType.DMA((192,)),
            pltpu.SemaphoreType.DMA((10,)),
        ],
        compiler_params=pltpu.CompilerParams(
            collective_id=0, has_side_effects=True, vmem_limit_bytes=48 << 20
        ),
    )(*operands)
    return pl.pallas_call(
        write_out,
        out_shape=tuple(jax.ShapeDtypeStruct(a.shape, a.dtype) for a in updated),
        in_specs=[any_] * 4,
        out_specs=(any_,) * 4,
        scratch_shapes=[pltpu.SemaphoreType.DMA((4,))],
        compiler_params=pltpu.CompilerParams(vmem_limit_bytes=1 << 20),
    )(*updated)


def solution(mesh):
    return jax.shard_map(
        per_device,
        mesh=mesh,
        in_specs=(
            P("pop", None, "wa"),
            P("pop", None, "wa"),
            P("pop"),
            P("pop"),
            P(("wa", "pop"), None),
            P(("wa", "pop"), None),
            P(("wa", "pop"), None),
        ),
        out_specs=(
            P(("wa", "pop"), None),
            P(("wa", "pop"), None),
            P(("wa", "pop"), None),
            P("wa", None),
        ),
        check_vma=False,
    )
```

```python
import math

import jax
import jax.numpy as jnp
from jax import lax
from jax.experimental import pallas as pl
from jax.experimental.pallas import tpu as pltpu
from jax.sharding import PartitionSpec as P

R = 4
STEP = 3
NZ, NYL, NX = 8, 2, 4
PLACE = [0, 1, 7, 2, 6, 3, 5, 4]
MESH = pl.DeviceIdType.MESH
F32 = jnp.float32
BF16 = jnp.bfloat16


def kernel(
    left_hbm, right_hbm, rank_hbm, sign_hbm, master_hbm, moment_hbm, second_hbm,
    out_master, out_moment, out_second, out_weights,
    rank_ref, sign_ref, left_raw, left_scaled, right, scale, adam_in,
    grad_p, grad_q, recv_p1, recv_p2, recv_q1, recv_q2, recv_y,
    state_send, state_recv, result_send, result_recv, rows_f32,
    gather_p, gather_q,
    send_sems, recv_sems, local_sems,
):
    members = rank_hbm.shape[0]
    depth = members * R
    pop = lax.axis_index("pop")
    wa = lax.axis_index("wa")
    z, yl, x = pop // (NYL * NX), lax.rem(pop // NX, NYL), lax.rem(pop, NX)
    yh, core = wa // 2, lax.rem(wa, 2)
    population = members * NZ * NYL * NX

    def flip(bit, by):
        return 1 - bit if by else bit

    def device(z_, yl_, x_, yh_, core_):
        return (z_ * (NYL * NX) + yl_ * NX + x_, yh_ * 2 + core_)

    def z_peer(step):
        return device(lax.rem(z + step + NZ, NZ), yl, x, yh, core)

    def x_peer(step):
        return device(z, yl, lax.rem(x + step + NX, NX), yh, core)

    def y_peer(phase, part, half):
        return device(z, flip(yl, half), x, flip(yh, phase), flip(core, part))

    others = [(a, b, c) for a in range(2) for b in range(2) for c in range(2) if a + b + c]
    plane = [(k, flip_y) for flip_y in range(2) for k in (2, 1, 3, 0) if k + flip_y]

    def plane_peer(k, flip_y):
        return device(z, flip(yl, flip_y), lax.rem(x + k, NX), yh, core)

    peers = [y_peer(*o) for o in others] + [z_peer(k) for k in range(1, NZ)]
    peers += [plane_peer(*o) for o in plane if o[0]]

    messages = []

    def send(src, dst, to):
        index = len(messages)
        message = pltpu.make_async_remote_copy(
            src_ref=src, dst_ref=dst, send_sem=send_sems.at[index],
            recv_sem=recv_sems.at[index], device_id=to, device_id_type=MESH,
        )
        message.start()
        messages.append(message)
        return message

    left_view = left_hbm.reshape(depth, left_hbm.shape[2])
    right_view = right_hbm.reshape(depth, right_hbm.shape[2])
    load_left = pltpu.make_async_copy(left_view, left_raw.at[0], local_sems.at[0])
    load_left.start()
    load_fitness = [
        pltpu.make_async_copy(rank_hbm, rank_ref, local_sems.at[8]),
        pltpu.make_async_copy(sign_hbm, sign_ref, local_sems.at[9]),
    ]
    load_right = []
    for c in range(NX):
        load_right.append(
            pltpu.make_async_copy(
                right_view.at[:, pl.ds(c * 256, 256)], right.at[c], local_sems.at[1 + c]
            )
        )
    load_state = [
        pltpu.make_async_copy(ref, adam_in.at[a], local_sems.at[5 + a])
        for a, ref in enumerate((master_hbm, moment_hbm, second_hbm))
    ]

    for copy in load_fitness + load_right + load_state:
        copy.start()

    barrier = pltpu.get_barrier_semaphore()
    for peer in peers:
        pl.semaphore_signal(barrier, inc=1, device_id=peer, device_id_type=MESH)
    pl.semaphore_wait(barrier, len(peers))

    halves = [pl.ds(0, depth // 2), pl.ds(depth // 2, depth // 2)]
    to_chip = [
        send(left_view.at[rows], left_raw.at[2, rows], y_peer(1, 0, 0)) for rows in halves
    ]
    to_core = send(left_view, left_raw.at[1], y_peer(0, 1, 0))
    for copy in load_fitness:
        copy.wait()

    square_sum = population * (population + 1) / (3.0 * (population - 1))
    norm = 1.0 / ((population - 1) * math.sqrt(square_sum * R))
    upper = lax.broadcasted_iota(jnp.int32, (8, 128), 0) < R

    def fill(j, _):
        def centred(m):
            return (2 * rank_ref[m] - (population - 1)) * (1 - 2 * sign_ref[m])

        first, second_ = centred(2 * j), centred(2 * j + 1)
        both = jnp.where(upper, jnp.full((8, 128), first), jnp.full((8, 128), second_))
        scale[pl.ds(pl.multiple_of(8 * j, 8), 8), :] = both.astype(F32) * norm
        return 0

    lax.fori_loop(0, members // 2, fill, 0, unroll=8)

    def product(slot, phase, part):
        def scaling(k, _):
            rows = pl.ds(pl.multiple_of(k * 128, 128), 128)
            factor = scale[rows, :]
            for half in range(2):
                cols = pl.ds(half * 128, 128)
                left_scaled[slot, rows, cols] = (
                    left_raw[slot, rows, cols].astype(F32) * factor
                ).astype(BF16)
            return 0

        lax.fori_loop(0, depth // 128, scaling, 0, unroll=True)

        def columns(c, _):
            block = lax.dot_general(
                left_scaled[slot], right[c], (((0,), (0,)), ((), ())),
                preferred_element_type=F32,
            )
            for zz in range(NZ):
                for yy in range(NYL):
                    half = 1 - yl if yy else yl
                    at = zz * 32 + yy * 16
                    piece = block[at : at + 16, :]
                    if part == phase:
                        grad_p[phase, half, zz, c] = piece
                    else:
                        grad_q[phase, half, c, zz] = piece
            return 0

        lax.fori_loop(0, NX, columns, 0, unroll=True)

    def ring_sum(chunks, slots, first_slot, size, me, peer, half):
        long = 1 if half == 0 else -1
        lanes = []
        slot = first_slot
        for direction in (long, -long):
            steps = size // 2 if direction == long else size // 2 - 1
            lanes.append((direction, steps, slot))
            slot += steps
        pending = {}

        def chunk(direction, distance):
            return lax.rem(me + direction * distance + size, size)

        for direction, steps, slot in lanes:
            pending[direction] = send(
                chunks.at[chunk(direction, steps)], slots.at[slot], peer(direction)
            )
        yield
        for j in range(1, size // 2 + 1):
            for direction, steps, slot in lanes:
                if j > steps:
                    continue
                pending[direction].wait_recv()
                target = chunk(direction, steps - j)
                chunks[target] = chunks[target] + slots[slot + j - 1]
                if j < steps:
                    pending[direction] = send(
                        chunks.at[target], slots.at[slot + j], peer(direction)
                    )
            if j < size // 2:
                yield

    def direct_sum(chunks, slots, size, me, peer):
        sent = []
        for k in sorted(range(1, size), key=lambda k: -min(k, size - k)):
            sent.append(
                send(chunks.at[lax.rem(me + k, size)], slots.at[k - 1], peer(k))
            )
        yield
        for message in sent:
            message.wait_recv()
        total = chunks[me]
        for k in range(1, size):
            total = total + slots[k - 1]
        chunks[me] = total

    exchanged = {}

    def reduction(phase, part, half):
        if part == phase:
            own = grad_p.at[phase, half]
            yield from ring_sum(own, recv_p1.at[phase, half], 0, NZ, z, z_peer, half)
            own = own.at[z]
            yield from direct_sum(own, recv_p2.at[phase, half], NX, x, x_peer)
            own = own.at[x]
        else:
            own = grad_q.at[phase, half]
            yield from ring_sum(own, recv_q1.at[phase, half], 0, NX, x, x_peer, half)
            own = own.at[x]
            yield from direct_sum(own, recv_q2.at[phase, half], NZ, z, z_peer)
            own = own.at[z]
        if phase + part + half:
            exchanged[phase, part, half] = send(
                own, recv_y.at[phase, part, half], y_peer(phase, part, half)
            )

    def step(tasks):
        for task in tasks:
            next(task, None)

    def begin(phase, part):
        tasks = [reduction(phase, part, half) for half in range(2)]
        step(tasks)
        return tasks

    load_left.wait()
    for copy in load_right:
        copy.wait()
    product(0, 0, 0)
    p0 = begin(0, 0)
    to_core.wait_recv()
    product(1, 0, 1)
    q0 = begin(0, 1)

    for copy in load_state:
        copy.wait()
    for xx in range(NX):
        for w in range(4):
            for a in range(3):
                state_send[xx, w, a] = adam_in[a, :, pl.ds(w * 1024 + xx * 256, 256)]
    state_recv[x] = state_send[x]
    state = []
    for k in (1, 2, 3):
        state.append(send(state_send.at[lax.rem(x + k, NX)], state_recv.at[x], x_peer(k)))

    for tasks in (p0, q0, p0, q0):
        step(tasks)
    to_core2 = []
    for message, rows in zip(to_chip, halves):
        message.wait_recv()
        to_core2.append(
            send(left_raw.at[2, rows], left_raw.at[3, rows], y_peer(0, 1, 0))
        )
    product(2, 1, 0)
    q1 = begin(1, 0)
    step(p0)
    for message in to_core2:
        message.wait_recv()
    product(3, 1, 1)
    p1 = begin(1, 1)

    for message in state:
        message.wait_recv()
    correct_one = 1.0 - 0.8**STEP
    correct_two = 1.0 - 0.95**STEP

    blocks = (gather_p, gather_q)
    columns_sent = ({}, {})
    result = []

    def return_results(phase):
        for k in (1, 2, 3):
            to = result_recv.at[phase, x]
            result.append(send(result_send.at[phase, lax.rem(x + k, NX)], to, x_peer(k)))
        result_recv[phase, x] = result_send[phase, x]

    def update(phase):
        for part in range(2):
            owner = flip(yh, phase) * 2 + flip(core, part)
            for half in range(2):
                if phase + part + half:
                    exchanged[phase, part, half].wait_recv()
            if phase + part == 0:
                gradient = grad_p[0, 0, z, x]
            else:
                gradient = recv_y[phase, part, 0]
            gradient = gradient + recv_y[phase, part, 1]
            for xx in range(NX):
                g = gradient[4 * xx : 4 * xx + 4, :]
                old_master = state_recv[xx, owner, 0]
                old_moment = state_recv[xx, owner, 1]
                old_second = state_recv[xx, owner, 2]
                new_moment = 0.8 * old_moment + 0.2 * g
                new_second = 0.95 * old_second + 0.05 * g * g
                new_master = old_master - 0.3 * (new_moment / correct_one) / (
                    jnp.sqrt(new_second / correct_two) + 1e-08
                )
                result_send[phase, xx, part, 0] = new_master
                result_send[phase, xx, part, 1] = new_moment
                result_send[phase, xx, part, 2] = new_second
                rows_f32[4 * xx : 4 * xx + 4, :] = new_master
            rounded = rows_f32[...].astype(BF16)
            blocks[phase][x, yl, 0, part] = rounded
        for k in (4, 3, 5, 2, 6, 1, 7):
            own = blocks[phase].at[x, yl, 0]
            to = blocks[phase].at[x, yl, PLACE.index(NZ - k)]
            columns_sent[phase][NZ - k] = send(own, to, z_peer(k))

    def spread(phase, first, count):
        for distance in PLACE[first : first + count]:
            if distance:
                columns_sent[phase][distance].wait_recv()
        own = blocks[phase].at[x, yl, pl.ds(first, count)]
        return [send(own, own, plane_peer(k, flip_y)) for k, flip_y in plane]

    def place(phase):
        for part in range(2):
            owner = flip(yh, phase) * 2 + flip(core, part)
            for distance in range(NZ):
                first_row = lax.rem(z + distance, NZ) * 32

                def put(xx, _):
                    cols = pl.ds(pl.multiple_of(owner * 1024 + xx * 256, 256), 256)
                    for yy in range(NYL):
                        rows = pl.ds(pl.multiple_of(first_row + yy * 16, 16), 16)
                        block = blocks[phase][xx, yy, PLACE.index(distance), part]
                        out_weights[rows, cols] = block
                    return 0

                lax.fori_loop(0, NX, put, 0, unroll=True)

    def gather0():
        update(0)
        yield
        gathered.extend(spread(0, 0, NZ))
        return_results(0)

    gathered = []
    g0 = [gather0()]
    for tasks in (p0, q0, p0, p1, q1, g0, p1, q1, g0, p1, p1, q1, p1):
        step(tasks)
    update(1)
    last = spread(1, 0, 1)
    last += spread(1, 1, 2)
    last += spread(1, 3, 5)
    return_results(1)
    for message in gathered:
        message.wait_recv()
    place(0)
    for message in last:
        message.wait_recv()
    place(1)

    for message in result:
        message.wait_recv()
    for xx in range(NX):
        for phase in range(2):
            for part in range(2):
                owner = flip(yh, phase) * 2 + flip(core, part)
                cols = pl.ds(pl.multiple_of(owner * 1024 + xx * 256, 256), 256)
                out_master[:, cols] = result_recv[phase, xx, part, 0]
                out_moment[:, cols] = result_recv[phase, xx, part, 1]
                out_second[:, cols] = result_recv[phase, xx, part, 2]

    for message in messages:
        message.wait_send()


def write_out(*refs):
    ins, outs, sems = refs[:4], refs[4:8], refs[8]
    copies = [pltpu.make_async_copy(ins[i], outs[i], sems.at[i]) for i in range(4)]
    for copy in reversed(copies):
        copy.start()
    for copy in copies:
        copy.wait()


def per_device(left_factors, right_factors, fitness_rank, sign_index, master, moment, second):
    members = left_factors.shape[0]
    depth = members * R
    hbm = pl.BlockSpec(memory_space=pltpu.HBM)
    any_ = pl.BlockSpec(memory_space=pl.ANY)
    vmem = pl.BlockSpec(memory_space=pltpu.VMEM)
    operands = [
        pltpu.with_memory_space_constraint(a, pltpu.HBM)
        for a in (left_factors, right_factors, fitness_rank, sign_index, master, moment, second)
    ]
    updated = pl.pallas_call(
        kernel,
        out_shape=(
            jax.ShapeDtypeStruct(master.shape, F32),
            jax.ShapeDtypeStruct(master.shape, F32),
            jax.ShapeDtypeStruct(master.shape, F32),
            jax.ShapeDtypeStruct((256, 4096), BF16),
        ),
        in_specs=[hbm] * 7,
        out_specs=(vmem, vmem, vmem, vmem),
        scratch_shapes=[
            pltpu.SMEM((members,), jnp.int32),
            pltpu.SMEM((members,), jnp.int32),
            pltpu.VMEM((4, depth, 256), BF16),
            pltpu.VMEM((4, depth, 256), BF16),
            pltpu.VMEM((NX, depth, 256), BF16),
            pltpu.VMEM((depth, 128), F32),
            pltpu.VMEM((3, 4, 4096), F32),
            pltpu.VMEM((2, 2, NZ, NX, 16, 256), F32),
            pltpu.VMEM((2, 2, NX, NZ, 16, 256), F32),
            pltpu.VMEM((2, 2, 7, NX, 16, 256), F32),
            pltpu.VMEM((2, 2, 3, 16, 256), F32),
            pltpu.VMEM((2, 2, 3, NZ, 16, 256), F32),
            pltpu.VMEM((2, 2, 7, 16, 256), F32),
            pltpu.VMEM((2, 2, 2, 16, 256), F32),
            pltpu.VMEM((NX, 4, 3, 4, 256), F32),
            pltpu.VMEM((NX, 4, 3, 4, 256), F32),
            pltpu.VMEM((2, NX, 2, 3, 4, 256), F32),
            pltpu.VMEM((2, NX, 2, 3, 4, 256), F32),
            pltpu.VMEM((16, 256), F32),
            pltpu.VMEM((NX, NYL, NZ, 2, 16, 256), BF16),
            pltpu.VMEM((NX, NYL, NZ, 2, 16, 256), BF16),
            pltpu.SemaphoreType.DMA((192,)),
            pltpu.SemaphoreType.DMA((192,)),
            pltpu.SemaphoreType.DMA((10,)),
        ],
        compiler_params=pltpu.CompilerParams(
            collective_id=0, has_side_effects=True, vmem_limit_bytes=48 << 20
        ),
    )(*operands)
    return pl.pallas_call(
        write_out,
        out_shape=tuple(jax.ShapeDtypeStruct(a.shape, a.dtype) for a in updated),
        in_specs=[any_] * 4,
        out_specs=(any_,) * 4,
        scratch_shapes=[pltpu.SemaphoreType.DMA((4,))],
        compiler_params=pltpu.CompilerParams(vmem_limit_bytes=1 << 20),
    )(*updated)


def solution(mesh):
    return jax.shard_map(
        per_device,
        mesh=mesh,
        in_specs=(
            P("pop", None, "wa"),
            P("pop", None, "wa"),
            P("pop"),
            P("pop"),
            P(("wa", "pop"), None),
            P(("wa", "pop"), None),
            P(("wa", "pop"), None),
        ),
        out_specs=(
            P(("wa", "pop"), None),
            P(("wa", "pop"), None),
            P(("wa", "pop"), None),
            P("wa", None),
        ),
        check_vma=False,
    )
```

```python
import math

import jax
import jax.numpy as jnp
from jax import lax
from jax.experimental import pallas as pl
from jax.experimental.pallas import tpu as pltpu
from jax.sharding import PartitionSpec as P

R = 4
STEP = 3
NZ, NYL, NX = 8, 2, 4
PLACE = [0, 1, 7, 2, 6, 3, 5, 4]
MESH = pl.DeviceIdType.MESH
F32 = jnp.float32
BF16 = jnp.bfloat16


def kernel(
    left_hbm, right_hbm, rank_hbm, sign_hbm, master_hbm, moment_hbm, second_hbm,
    out_master, out_moment, out_second, out_weights,
    rank_ref, sign_ref, left_raw, left_scaled, right, scale, adam_in,
    grad_p, grad_q, recv_p1, recv_p2, recv_q1, recv_q2, recv_y,
    state_send, state_recv, result_send, result_recv, rows_f32,
    gather_p, gather_q,
    send_sems, recv_sems, local_sems,
):
    members = rank_hbm.shape[0]
    depth = members * R
    pop = lax.axis_index("pop")
    wa = lax.axis_index("wa")
    z, yl, x = pop // (NYL * NX), lax.rem(pop // NX, NYL), lax.rem(pop, NX)
    yh, core = wa // 2, lax.rem(wa, 2)
    population = members * NZ * NYL * NX

    def flip(bit, by):
        return 1 - bit if by else bit

    def device(z_, yl_, x_, yh_, core_):
        return (z_ * (NYL * NX) + yl_ * NX + x_, yh_ * 2 + core_)

    def z_peer(step):
        return device(lax.rem(z + step + NZ, NZ), yl, x, yh, core)

    def x_peer(step):
        return device(z, yl, lax.rem(x + step + NX, NX), yh, core)

    def y_peer(phase, part, half):
        return device(z, flip(yl, half), x, flip(yh, phase), flip(core, part))

    others = [(a, b, c) for a in range(2) for b in range(2) for c in range(2) if a + b + c]
    plane = [(k, flip_y) for flip_y in range(2) for k in (2, 1, 3, 0) if k + flip_y]

    def plane_peer(k, flip_y):
        return device(z, flip(yl, flip_y), lax.rem(x + k, NX), yh, core)

    peers = [z_peer(k) for k in (4, 3, 5, 2, 6, 1, 7)]
    peers += [plane_peer(*o) for o in reversed(plane) if o[0]]
    peers += [y_peer(*o) for o in reversed(others)]

    messages = []

    def send(src, dst, to):
        index = len(messages)
        message = pltpu.make_async_remote_copy(
            src_ref=src, dst_ref=dst, send_sem=send_sems.at[index],
            recv_sem=recv_sems.at[index], device_id=to, device_id_type=MESH,
        )
        message.start()
        messages.append(message)
        return message

    left_view = left_hbm.reshape(depth, left_hbm.shape[2])
    right_view = right_hbm.reshape(depth, right_hbm.shape[2])
    load_left = pltpu.make_async_copy(left_view, left_raw.at[0], local_sems.at[0])
    load_left.start()
    load_fitness = [
        pltpu.make_async_copy(rank_hbm, rank_ref, local_sems.at[8]),
        pltpu.make_async_copy(sign_hbm, sign_ref, local_sems.at[9]),
    ]
    load_right = []
    for c in range(NX):
        load_right.append(
            pltpu.make_async_copy(
                right_view.at[:, pl.ds(c * 256, 256)], right.at[c], local_sems.at[1 + c]
            )
        )
    load_state = [
        pltpu.make_async_copy(ref, adam_in.at[a], local_sems.at[5 + a])
        for a, ref in enumerate((master_hbm, moment_hbm, second_hbm))
    ]

    for copy in load_fitness + load_right + load_state:
        copy.start()

    barrier = pltpu.get_barrier_semaphore()
    for peer in peers:
        pl.semaphore_signal(barrier, inc=1, device_id=peer, device_id_type=MESH)
    pl.semaphore_wait(barrier, len(peers))

    halves = [pl.ds(0, depth // 2), pl.ds(depth // 2, depth // 2)]
    to_chip = [
        send(left_view.at[rows], left_raw.at[2, rows], y_peer(1, 0, 0)) for rows in halves
    ]
    to_core = send(left_view, left_raw.at[1], y_peer(0, 1, 0))
    for copy in load_fitness:
        copy.wait()

    square_sum = population * (population + 1) / (3.0 * (population - 1))
    norm = 1.0 / ((population - 1) * math.sqrt(square_sum * R))
    upper = lax.broadcasted_iota(jnp.int32, (8, 128), 0) < R

    def fill(j, _):
        def centred(m):
            return (2 * rank_ref[m] - (population - 1)) * (1 - 2 * sign_ref[m])

        first, second_ = centred(2 * j), centred(2 * j + 1)
        both = jnp.where(upper, jnp.full((8, 128), first), jnp.full((8, 128), second_))
        scale[pl.ds(pl.multiple_of(8 * j, 8), 8), :] = both.astype(F32) * norm
        return 0

    lax.fori_loop(0, members // 2, fill, 0, unroll=8)

    def product(slot, phase, part):
        def scaling(k, _):
            rows = pl.ds(pl.multiple_of(k * 128, 128), 128)
            factor = scale[rows, :]
            for half in range(2):
                cols = pl.ds(half * 128, 128)
                left_scaled[slot, rows, cols] = (
                    left_raw[slot, rows, cols].astype(F32) * factor
                ).astype(BF16)
            return 0

        lax.fori_loop(0, depth // 128, scaling, 0, unroll=True)

        def columns(c, _):
            block = lax.dot_general(
                left_scaled[slot], right[c], (((0,), (0,)), ((), ())),
                preferred_element_type=F32,
            )
            for zz in range(NZ):
                for yy in range(NYL):
                    half = 1 - yl if yy else yl
                    at = zz * 32 + yy * 16
                    piece = block[at : at + 16, :]
                    if part == phase:
                        grad_p[phase, half, zz, c] = piece
                    else:
                        grad_q[phase, half, c, zz] = piece
            return 0

        lax.fori_loop(0, NX, columns, 0, unroll=True)

    def ring_sum(chunks, slots, first_slot, size, me, peer, half):
        long = 1 if half == 0 else -1
        lanes = []
        slot = first_slot
        for direction in (long, -long):
            steps = size // 2 if direction == long else size // 2 - 1
            lanes.append((direction, steps, slot))
            slot += steps
        pending = {}

        def chunk(direction, distance):
            return lax.rem(me + direction * distance + size, size)

        for direction, steps, slot in lanes:
            pending[direction] = send(
                chunks.at[chunk(direction, steps)], slots.at[slot], peer(direction)
            )
        yield
        for j in range(1, size // 2 + 1):
            for direction, steps, slot in lanes:
                if j > steps:
                    continue
                pending[direction].wait_recv()
                target = chunk(direction, steps - j)
                chunks[target] = chunks[target] + slots[slot + j - 1]
                if j < steps:
                    pending[direction] = send(
                        chunks.at[target], slots.at[slot + j], peer(direction)
                    )
            if j < size // 2:
                yield

    def direct_sum(chunks, slots, size, me, peer):
        sent = []
        for k in sorted(range(1, size), key=lambda k: -min(k, size - k)):
            sent.append(
                send(chunks.at[lax.rem(me + k, size)], slots.at[k - 1], peer(k))
            )
        yield
        for message in sent:
            message.wait_recv()
        total = chunks[me]
        for k in range(1, size):
            total = total + slots[k - 1]
        chunks[me] = total

    exchanged = {}

    def reduction(phase, part, half):
        if part == phase:
            own = grad_p.at[phase, half]
            yield from ring_sum(own, recv_p1.at[phase, half], 0, NZ, z, z_peer, half)
            own = own.at[z]
            yield from direct_sum(own, recv_p2.at[phase, half], NX, x, x_peer)
            own = own.at[x]
        else:
            own = grad_q.at[phase, half]
            yield from ring_sum(own, recv_q1.at[phase, half], 0, NX, x, x_peer, half)
            own = own.at[x]
            yield from direct_sum(own, recv_q2.at[phase, half], NZ, z, z_peer)
            own = own.at[z]
        if phase + part + half:
            exchanged[phase, part, half] = send(
                own, recv_y.at[phase, part, half], y_peer(phase, part, half)
            )

    def step(tasks):
        for task in tasks:
            next(task, None)

    def begin(phase, part):
        tasks = [reduction(phase, part, half) for half in range(2)]
        step(tasks)
        return tasks

    load_left.wait()
    for copy in load_right:
        copy.wait()
    product(0, 0, 0)
    p0 = begin(0, 0)
    to_core.wait_recv()
    product(1, 0, 1)
    q0 = begin(0, 1)

    for copy in load_state:
        copy.wait()
    for xx in range(NX):
        for w in range(4):
            for a in range(3):
                state_send[xx, w, a] = adam_in[a, :, pl.ds(w * 1024 + xx * 256, 256)]
    state_recv[x] = state_send[x]
    state = []
    for k in (1, 2, 3):
        state.append(send(state_send.at[lax.rem(x + k, NX)], state_recv.at[x], x_peer(k)))

    for tasks in (p0, q0, p0, q0):
        step(tasks)
    to_core2 = []
    for message, rows in zip(to_chip, halves):
        message.wait_recv()
        to_core2.append(
            send(left_raw.at[2, rows], left_raw.at[3, rows], y_peer(0, 1, 0))
        )
    product(2, 1, 0)
    q1 = begin(1, 0)
    step(p0)
    for message in to_core2:
        message.wait_recv()
    product(3, 1, 1)
    p1 = begin(1, 1)

    for message in state:
        message.wait_recv()
    correct_one = 1.0 - 0.8**STEP
    correct_two = 1.0 - 0.95**STEP

    blocks = (gather_p, gather_q)
    columns_sent = ({}, {})
    result = []

    def return_results(phase):
        for k in (1, 2, 3):
            to = result_recv.at[phase, x]
            result.append(send(result_send.at[phase, lax.rem(x + k, NX)], to, x_peer(k)))
        result_recv[phase, x] = result_send[phase, x]

    def update(phase):
        for part in range(2):
            owner = flip(yh, phase) * 2 + flip(core, part)
            for half in range(2):
                if phase + part + half:
                    exchanged[phase, part, half].wait_recv()
            if phase + part == 0:
                gradient = grad_p[0, 0, z, x]
            else:
                gradient = recv_y[phase, part, 0]
            gradient = gradient + recv_y[phase, part, 1]
            for xx in range(NX):
                g = gradient[4 * xx : 4 * xx + 4, :]
                old_master = state_recv[xx, owner, 0]
                old_moment = state_recv[xx, owner, 1]
                old_second = state_recv[xx, owner, 2]
                new_moment = 0.8 * old_moment + 0.2 * g
                new_second = 0.95 * old_second + 0.05 * g * g
                new_master = old_master - 0.3 * (new_moment / correct_one) / (
                    jnp.sqrt(new_second / correct_two) + 1e-08
                )
                result_send[phase, xx, part, 0] = new_master
                result_send[phase, xx, part, 1] = new_moment
                result_send[phase, xx, part, 2] = new_second
                rows_f32[4 * xx : 4 * xx + 4, :] = new_master
            rounded = rows_f32[...].astype(BF16)
            blocks[phase][x, yl, 0, part] = rounded
        for k in (4, 3, 5, 2, 6, 1, 7):
            own = blocks[phase].at[x, yl, 0]
            to = blocks[phase].at[x, yl, PLACE.index(NZ - k)]
            columns_sent[phase][NZ - k] = send(own, to, z_peer(k))

    def spread(phase, first, count):
        for distance in PLACE[first : first + count]:
            if distance:
                columns_sent[phase][distance].wait_recv()
        own = blocks[phase].at[x, yl, pl.ds(first, count)]
        return [send(own, own, plane_peer(k, flip_y)) for k, flip_y in plane]

    def place(phase):
        for part in range(2):
            owner = flip(yh, phase) * 2 + flip(core, part)
            for distance in range(NZ):
                first_row = lax.rem(z + distance, NZ) * 32

                def put(xx, _):
                    cols = pl.ds(pl.multiple_of(owner * 1024 + xx * 256, 256), 256)
                    for yy in range(NYL):
                        rows = pl.ds(pl.multiple_of(first_row + yy * 16, 16), 16)
                        block = blocks[phase][xx, yy, PLACE.index(distance), part]
                        out_weights[rows, cols] = block
                    return 0

                lax.fori_loop(0, NX, put, 0, unroll=True)

    def gather0():
        update(0)
        yield
        gathered.extend(spread(0, 0, NZ))
        return_results(0)

    gathered = []
    g0 = [gather0()]
    for tasks in (p0, q0, p0, p1, q1, g0, p1, q1, g0, p1, p1, q1, p1):
        step(tasks)
    update(1)
    last = spread(1, 0, 1)
    last += spread(1, 1, 2)
    last += spread(1, 3, 5)
    return_results(1)
    for message in gathered:
        message.wait_recv()
    place(0)
    for message in last:
        message.wait_recv()
    place(1)

    for message in result:
        message.wait_recv()
    for xx in range(NX):
        for phase in range(2):
            for part in range(2):
                owner = flip(yh, phase) * 2 + flip(core, part)
                cols = pl.ds(pl.multiple_of(owner * 1024 + xx * 256, 256), 256)
                out_master[:, cols] = result_recv[phase, xx, part, 0]
                out_moment[:, cols] = result_recv[phase, xx, part, 1]
                out_second[:, cols] = result_recv[phase, xx, part, 2]

    for message in messages:
        message.wait_send()


def write_out(*refs):
    ins, outs, sems = refs[:4], refs[4:8], refs[8]
    copies = [pltpu.make_async_copy(ins[i], outs[i], sems.at[i]) for i in range(4)]
    for copy in reversed(copies):
        copy.start()
    for copy in copies:
        copy.wait()


def per_device(left_factors, right_factors, fitness_rank, sign_index, master, moment, second):
    members = left_factors.shape[0]
    depth = members * R
    hbm = pl.BlockSpec(memory_space=pltpu.HBM)
    any_ = pl.BlockSpec(memory_space=pl.ANY)
    vmem = pl.BlockSpec(memory_space=pltpu.VMEM)
    operands = [
        pltpu.with_memory_space_constraint(a, pltpu.HBM)
        for a in (left_factors, right_factors, fitness_rank, sign_index, master, moment, second)
    ]
    updated = pl.pallas_call(
        kernel,
        out_shape=(
            jax.ShapeDtypeStruct(master.shape, F32),
            jax.ShapeDtypeStruct(master.shape, F32),
            jax.ShapeDtypeStruct(master.shape, F32),
            jax.ShapeDtypeStruct((256, 4096), BF16),
        ),
        in_specs=[hbm] * 7,
        out_specs=(vmem, vmem, vmem, vmem),
        scratch_shapes=[
            pltpu.SMEM((members,), jnp.int32),
            pltpu.SMEM((members,), jnp.int32),
            pltpu.VMEM((4, depth, 256), BF16),
            pltpu.VMEM((4, depth, 256), BF16),
            pltpu.VMEM((NX, depth, 256), BF16),
            pltpu.VMEM((depth, 128), F32),
            pltpu.VMEM((3, 4, 4096), F32),
            pltpu.VMEM((2, 2, NZ, NX, 16, 256), F32),
            pltpu.VMEM((2, 2, NX, NZ, 16, 256), F32),
            pltpu.VMEM((2, 2, 7, NX, 16, 256), F32),
            pltpu.VMEM((2, 2, 3, 16, 256), F32),
            pltpu.VMEM((2, 2, 3, NZ, 16, 256), F32),
            pltpu.VMEM((2, 2, 7, 16, 256), F32),
            pltpu.VMEM((2, 2, 2, 16, 256), F32),
            pltpu.VMEM((NX, 4, 3, 4, 256), F32),
            pltpu.VMEM((NX, 4, 3, 4, 256), F32),
            pltpu.VMEM((2, NX, 2, 3, 4, 256), F32),
            pltpu.VMEM((2, NX, 2, 3, 4, 256), F32),
            pltpu.VMEM((16, 256), F32),
            pltpu.VMEM((NX, NYL, NZ, 2, 16, 256), BF16),
            pltpu.VMEM((NX, NYL, NZ, 2, 16, 256), BF16),
            pltpu.SemaphoreType.DMA((192,)),
            pltpu.SemaphoreType.DMA((192,)),
            pltpu.SemaphoreType.DMA((10,)),
        ],
        compiler_params=pltpu.CompilerParams(
            collective_id=0, has_side_effects=True, vmem_limit_bytes=48 << 20
        ),
    )(*operands)
    return pl.pallas_call(
        write_out,
        out_shape=tuple(jax.ShapeDtypeStruct(a.shape, a.dtype) for a in updated),
        in_specs=[any_] * 4,
        out_specs=(any_,) * 4,
        scratch_shapes=[pltpu.SemaphoreType.DMA((4,))],
        compiler_params=pltpu.CompilerParams(vmem_limit_bytes=1 << 20),
    )(*updated)


def solution(mesh):
    return jax.shard_map(
        per_device,
        mesh=mesh,
        in_specs=(
            P("pop", None, "wa"),
            P("pop", None, "wa"),
            P("pop"),
            P("pop"),
            P(("wa", "pop"), None),
            P(("wa", "pop"), None),
            P(("wa", "pop"), None),
        ),
        out_specs=(
            P(("wa", "pop"), None),
            P(("wa", "pop"), None),
            P(("wa", "pop"), None),
            P("wa", None),
        ),
        check_vma=False,
    )
```
